32 devices in a mesh: row: 8 (over z, core), col: 4 (over y, x).
Axes of the slice: x: 2, y: 2, z: 4, core: 2. Of those that a mesh axis runs over, the one named last changes fastest.
Arguments:
- slab: float32 [16384, 1024], P('row', 'col'), may hold values from -6 to 6
- ranks: int32 [2, 1024], P(None, 'col'), may hold values from 0 to 1023, as said below
- poles: float32 [2, 1024], P(None, 'col'), as said below
- roots: float32 [2, 1024], P(None, 'col')
- flags: int32 [2, 1024], P(None, 'col'), may hold values 0 or 1
- reflectors: float32 [8, 16384], P(None, 'row'), may hold values from -0.5 to 0.5
- reflector_scales: float32 [8, 128], P(None, 'row'), may hold values from 1 to 1.6
Outputs:
- eigenvectors: float32 [16384, 1024], P('row', 'col')
The draws below stay inside these ranges and needn't reach their ends.
Inputs may be any that keep to these rules, and one draw needn't show every extreme that they name: Within each aligned group of 512 entries of level one, and of 1024 entries of level two, the ranks are a permutation of the group's positions. At each level, every root differs from every pole of its group by 0.05 or more, and two poles of one group differ by 0.6 or more.
All inputs are finite; a program needn't handle non-finite values. No bound on the sum of `flags` on one device may be relied on, other than what follows from the above.
Results may differ from the reference program's by a relative error of at most 0.0003.
Values sent between devices are 32-bit elements; how exact they have to be, the bound alone decides.
A program may use at most 64 MiB of HBM per device.

```python
from functools import partial
import jax
import jax.numpy as jnp
from jax import lax

BAND = 128
SETS = 8
ORDER = 16384
SLAB = 1024
GROUP_ONE = 512
GROUP_TWO = 1024
WINDOWS = 128


def column_ranks(key):
    levels = []
    for level, group_size in ((0, GROUP_ONE), (1, GROUP_TWO)):
        group_keys = jax.random.split(jax.random.fold_in(key, 7 + level), SLAB // group_size)
        shuffled = jax.vmap(partial(jax.random.permutation, x=group_size))(group_keys)
        levels.append(shuffled.reshape(SLAB).astype(jnp.int32))
    return jnp.stack(levels)


def draw_ranks(key, part):
    return column_ranks(key)


def draw_poles(key, part):
    centres = column_ranks(key).astype(jnp.float32)
    jitter_key = jax.random.fold_in(key, 31)
    jitter = jax.random.uniform(jitter_key, centres.shape, jnp.float32, -0.2, 0.2)
    return centres + jitter


def draw_roots(key, part):
    positions = jnp.arange(SLAB, dtype=jnp.int32)
    centres = jnp.stack([(positions % GROUP_ONE).astype(jnp.float32), (positions % GROUP_TWO).astype(jnp.float32)])
    frac_key = jax.random.fold_in(key, 41)
    fraction = jax.random.uniform(frac_key, centres.shape, jnp.float32, 0.25, 0.75)
    return centres + fraction


def plant(values, stream_key, low, high):
    spot = [jax.random.randint(jax.random.fold_in(stream_key, axis), (), 0, length) for axis, length in enumerate(values.shape)]
    longest = values.shape.index(max(values.shape))
    beside = spot[:longest] + [(spot[longest] + 1) % values.shape[longest]] + spot[longest + 1:]
    return values.at[tuple(spot)].set(low).at[tuple(beside)].set(high)


def level_of(stream_key, shape, cuts, smallest, largest):
    level = 1.0
    for dim, blocks in cuts:
        steps = jax.random.uniform(jax.random.fold_in(jax.random.fold_in(stream_key, 6), dim), (blocks,), jnp.float32, smallest / len(cuts), largest / len(cuts))
        level = level * jnp.repeat(jnp.exp(steps), shape[dim] // blocks).reshape((-1,) + (1,) * (len(shape) - 1 - dim))
    return level


def centred(own_key, extent, width, limit, cuts=(), kind=jnp.bfloat16):
    level = level_of(own_key, extent, cuts, -0.22, 0.18) if cuts else 1.0
    array = jax.random.normal(own_key, extent, jnp.float32) * width * level
    return jnp.minimum(jnp.maximum(array, -limit), limit).astype(kind)


def setup_inputs(seed: int = 0) -> dict:
    key_of = jax.random.split(jax.random.key(seed), 8)
    return {
        "slab": centred(key_of[0], (ORDER, SLAB), 1.0, 6.0, ((0, 8), (1, 4)), jnp.float32),
        "ranks": draw_ranks(jax.random.fold_in(key_of[7], 71), 0),
        "poles": draw_poles(jax.random.fold_in(key_of[7], 71), 0),
        "roots": draw_roots(jax.random.fold_in(key_of[7], 71), 0),
        "flags": plant((jax.random.randint(key_of[4], (2, SLAB), 0, 4) < 1).astype(jnp.int32), jax.random.fold_in(key_of[4], 1), 0, 1),
        "reflectors": centred(key_of[5], (SETS, ORDER), BAND ** -0.5, 0.5, ((1, 8),), jnp.float32),
        "reflector_scales": jnp.clip(1.0 + 0.6 * jax.random.uniform(key_of[6], (SETS, WINDOWS), jnp.float32) ** level_of(key_of[6], (SETS, WINDOWS), ((1, 8),), -0.2, 0.2), 1.0, 1.6),
    }


exact_precision = lax.Precision.HIGHEST

def set_offset(index):
    return 1 + (SETS - 1 - index) * (BAND - 2) // (SETS - 1)

def loewner(group_ranks, group_poles, group_roots, group_flags, rank_start, rank_count):
    group_size = group_poles.shape[0]
    living = (1 - group_flags).astype(jnp.float32)
    root_of = jnp.take(group_roots, group_ranks)
    to_root = jnp.abs(root_of[None, :] - group_poles[:, None])
    between = jnp.abs(group_poles[None, :] - group_poles[:, None])
    diagonal_mask = lax.broadcasted_iota(jnp.int32, (group_size, group_size), 0) == lax.broadcasted_iota(jnp.int32, (group_size, group_size), 1)
    ratios = to_root / jnp.where(diagonal_mask, 1.0, between)
    weights = jnp.exp(0.5 * lax.optimization_barrier(jnp.sum(living[None, :] * jnp.log(ratios), axis=1)))
    picked = lax.dynamic_slice_in_dim(group_roots, rank_start, rank_count)
    cauchy = (living * weights)[:, None] / (group_poles[:, None] - picked[None, :])
    column_norms = jnp.sqrt(lax.optimization_barrier(jnp.sum(cauchy * cauchy, axis=0)))
    rank_cols = rank_start + lax.broadcasted_iota(jnp.int32, (group_size, rank_count), 1)
    matches = group_ranks[:, None] == rank_cols
    rank_dead = lax.optimization_barrier(jnp.sum(jnp.where(matches, group_flags[:, None], 0), axis=0)) > 0
    return jnp.where(rank_dead[None, :], matches.astype(cauchy.dtype), cauchy / column_norms[None, :])

def merge_level(matrix, level_ranks, level_poles, level_roots, level_flags, group_size):
    row_count = matrix.shape[0]
    groups = matrix.shape[1] // group_size
    blocks = matrix.reshape(row_count, groups, group_size).transpose(1, 0, 2)

    def one_group(pieces):
        block_cols, group_ranks, group_poles, group_roots, group_flags = pieces
        mixing = loewner(group_ranks, group_poles, group_roots, group_flags, 0, group_size)
        return jnp.dot(block_cols, mixing, precision=exact_precision, preferred_element_type=jnp.float32)
    merged = lax.map(one_group, (blocks, level_ranks.reshape(groups, group_size), level_poles.reshape(groups, group_size), level_roots.reshape(groups, group_size), level_flags.reshape(groups, group_size)))
    return merged.transpose(1, 0, 2).reshape(row_count, groups * group_size)

def reflect(matrix, vector, scales, offset):
    total = matrix.shape[0]
    tile_count = total // BAND
    head_rows = matrix[:offset]
    padded = jnp.concatenate([matrix[offset:], jnp.zeros((offset, matrix.shape[1]), matrix.dtype)], axis=0)
    vectors = jnp.concatenate([vector[offset:], jnp.zeros((offset,), vector.dtype)]).reshape(tile_count, BAND)
    panels = padded.reshape(tile_count, BAND, matrix.shape[1])
    projections = jnp.einsum('kb,kbc->kc', vectors, panels, precision=exact_precision)
    panels = panels - (scales[:, None] * projections)[:, None, :] * vectors[:, :, None]
    return jnp.concatenate([head_rows, panels.reshape(tile_count * BAND, matrix.shape[1])[:total - offset]], axis=0)

def reference(slab, ranks, poles, roots, flags, reflectors, reflector_scales):
    matrix = merge_level(slab, ranks[0], poles[0], roots[0], flags[0], GROUP_ONE)
    matrix = merge_level(matrix, ranks[1], poles[1], roots[1], flags[1], GROUP_TWO)
    for index in range(SETS):
        matrix = reflect(matrix, reflectors[index], reflector_scales[index], set_offset(index))
    return matrix
```

```python
import functools

import jax
import jax.numpy as jnp
from jax import lax
from jax.experimental import pallas as pl
from jax.experimental.pallas import tpu as pltpu
from jax.sharding import PartitionSpec as P

BAND = 128
SETS = 8
ABOVE = 1024
BELOW = 128
CHUNK = 256
MESH = pl.DeviceIdType.MESH
F32 = jnp.float32
BF16 = jnp.bfloat16


def set_offset(index):
    return 1 + (SETS - 1 - index) * (BAND - 2) // (SETS - 1)


def halves(value):
    high = value.astype(BF16)
    low = (value - high.astype(F32)).astype(BF16)
    return high, low


def dot(left, right):
    return jnp.dot(left, right, preferred_element_type=F32)


def dot3(left, right_high, right_low):
    high, low = halves(left)
    return dot(high, right_high) + (dot(high, right_low) + dot(low, right_high))


def kernel(
    slab, ranks, poles, roots, flags, reflectors, scales, out,
    ext, refl, scales_own, scales_above, turned, gathered, tables, tall, wide,
    raw_ints, raw_floats, picked, shared, spread_weights,
    mix_one, mix_two, plan_high, plan_low, partial, arrived,
    local_sems, halo_send, halo_recv, table_send, table_recv,
    weight_send, weight_recv, gather_send, gather_recv, reduce_send, reduce_recv,
):
    rows = slab.shape[0]
    width = slab.shape[1]
    chunks = rows // CHUNK
    windows = (rows + ABOVE) // BAND
    above_windows = ABOVE // BAND
    row = lax.axis_index("row")
    row_size = lax.axis_size("row")
    col = lax.axis_index("col")
    quarter = lax.rem(col, 4)
    quad = col - quarter
    near = quarter + 1 - 2 * lax.rem(quarter, 2)
    far = lax.rem(quarter + 2, 4)
    across = 3 - quarter
    near_id = (row, quad + near)
    far_id = (row, quad + far)
    across_id = (row, quad + across)
    has_prev = row > 0
    has_next = row < row_size - 1
    prev_id = (lax.max(row - 1, 0), col)
    next_id = (lax.min(row + 1, row_size - 1), col)

    own_rows = pl.ds(ABOVE, rows)
    own_slab = pltpu.make_async_copy(slab, ext.at[own_rows], local_sems.at[0])
    own_refl = pltpu.make_async_copy(reflectors, refl.at[:, own_rows], local_sems.at[1])
    own_scale_copy = pltpu.make_async_copy(scales, scales_own, local_sems.at[2])
    small = [
        pltpu.make_async_copy(ranks, raw_ints.at[0], local_sems.at[3]),
        pltpu.make_async_copy(flags, raw_ints.at[1], local_sems.at[4]),
        pltpu.make_async_copy(poles, raw_floats.at[0], local_sems.at[5]),
        pltpu.make_async_copy(roots, raw_floats.at[1], local_sems.at[6]),
    ]
    for copy in small:
        copy.start()
    own_refl.start()
    own_scale_copy.start()
    own_slab.start()

    barrier = pltpu.get_barrier_semaphore()
    for partner in (near_id, far_id, across_id):
        pl.semaphore_signal(barrier, inc=1, device_id=partner, device_id_type=MESH)

    @pl.when(has_prev)
    def _():
        pl.semaphore_signal(barrier, inc=1, device_id=prev_id, device_id_type=MESH)

    @pl.when(has_next)
    def _():
        pl.semaphore_signal(barrier, inc=1, device_id=next_id, device_id_type=MESH)

    for copy in small:
        copy.wait()
    tables[quarter] = jnp.concatenate(
        [raw_ints[0].astype(F32), raw_floats[0], raw_floats[1], raw_ints[1].astype(F32)], axis=0
    )

    pl.semaphore_wait(
        barrier, 3 + jnp.where(has_prev, 1, 0) + jnp.where(has_next, 1, 0)
    )

    def remote(source, target, send, recv, device):
        return pltpu.make_async_remote_copy(
            src_ref=source, dst_ref=target, send_sem=send, recv_sem=recv,
            device_id=device, device_id_type=MESH,
        )

    last = rows - ABOVE
    to_prev = [
        remote(reflectors.at[:, pl.ds(0, BELOW)], refl.at[:, pl.ds(ABOVE + rows, BELOW)],
               halo_send.at[0], halo_recv.at[0], prev_id),
        remote(slab.at[pl.ds(0, BELOW)], ext.at[pl.ds(ABOVE + rows, BELOW)],
               halo_send.at[1], halo_recv.at[1], prev_id),
    ]
    unread = set_offset(0) // 8 * 8
    to_next = [
        remote(slab.at[pl.ds(last + unread, ABOVE - unread)],
               ext.at[pl.ds(unread, ABOVE - unread)],
               halo_send.at[4], halo_recv.at[4], next_id),
        remote(reflectors.at[:, pl.ds(last, ABOVE)], refl.at[:, pl.ds(0, ABOVE)],
               halo_send.at[2], halo_recv.at[2], next_id),
        remote(scales, scales_above, halo_send.at[3], halo_recv.at[3], next_id),
    ]

    @pl.when(has_prev)
    def _():
        for copy in to_prev:
            copy.start()

    @pl.when(has_next)
    def _():
        for copy in to_next:
            copy.start()

    table_copies = [
        remote(tables.at[quarter], tables.at[quarter], table_send.at[i], table_recv.at[i], device)
        for i, device in enumerate((near_id, far_id, across_id))
    ]
    for copy in table_copies:
        copy.start()

    @pl.when(jnp.logical_not(has_prev))
    def _():
        ext[pl.ds(0, ABOVE)] = jnp.zeros((ABOVE, width), F32)
        refl[:, pl.ds(0, ABOVE)] = jnp.zeros((SETS, ABOVE), F32)
        scales_above[...] = jnp.zeros(scales_above.shape, F32)

    @pl.when(jnp.logical_not(has_next))
    def _():
        ext[pl.ds(ABOVE + rows, BELOW)] = jnp.zeros((BELOW, width), F32)
        refl[:, pl.ds(ABOVE + rows, BELOW)] = jnp.zeros((SETS, BELOW), F32)

    own_refl.wait()
    own_scale_copy.wait()
    own_slab.wait()

    @pl.when(has_next)
    def _():
        to_prev[0].wait_recv()
        to_prev[1].wait_recv()

    lane = lax.broadcasted_iota(jnp.int32, (SETS, BAND), 1)
    offsets = 1 + (SETS - 1 - lax.broadcasted_iota(jnp.int32, (SETS, BAND), 0)) * (
        (BAND - 2) // (SETS - 1)
    )

    def turn(block, low_scale, high_scale):
        spread = jnp.where(lane < offsets, low_scale, high_scale)
        both = jnp.concatenate([refl[:, block * BAND : (block + 1) * BAND], spread], axis=0)
        turned[block * BAND : (block + 1) * BAND, : 2 * SETS] = both.T

    own_scales = scales_own[...]

    def own_scale(window):
        index = min(max(window - above_windows, 0), own_scales.shape[1] - 1)
        return own_scales[:, index : index + 1]

    for block in range(above_windows, windows + 1):
        turn(block, own_scale(block - 1), own_scale(block))

    place = lax.broadcasted_iota(jnp.int32, (BAND + 8, 1), 0)

    def sweep(index, first, stop):
        offset = set_offset(index)
        base, shift = offset // 8 * 8, offset % 8
        inside = (place >= shift) & (place < BAND + shift)

        def window(w, carry):
            start = pl.multiple_of(w * BAND + base, 8)
            span = pl.ds(start, BAND + 8)
            blade = jnp.where(inside, turned[span, index : index + 1], 0.0)
            scale = turned[pl.ds(start + 8, 8), SETS + index : SETS + index + 1]
            panel = ext[span]
            projection = jnp.sum(blade * panel, axis=0, keepdims=True) * scale[:1]
            ext[span] = panel - blade * projection
            return carry

        lax.fori_loop(first, stop, window, 0, unroll=stop - first)

    def gather_copy(chunk, device):
        return remote(
            ext.at[pl.ds(ABOVE + chunk * CHUNK, CHUNK)],
            gathered.at[pl.ds(chunk * CHUNK, CHUNK)],
            gather_send.at[chunk], gather_recv.at[chunk], device,
        )

    def reduce_copy(chunk, device):
        span = pl.ds(chunk * CHUNK, CHUNK)
        return remote(
            partial.at[span], arrived.at[span],
            reduce_send.at[chunk], reduce_recv.at[chunk], device,
        )

    def send_chunk(chunk):
        gather_copy(chunk, near_id if chunk % 2 == 0 else far_id).start()

    half = ABOVE // CHUNK
    edge = above_windows + SETS
    for index in range(SETS):
        sweep(index, above_windows + index, edge + 2)
    send_chunk(half)
    first = edge + 2
    for chunk in range(half + 1, chunks):
        for index in range(SETS):
            sweep(index, first, first + CHUNK // BAND)
        first += CHUNK // BAND
        send_chunk(chunk)

    for copy in table_copies:
        copy.wait_recv()
    for i in range(4):
        wide[:, i * width : (i + 1) * width] = tables[i]
    for i in range(4 * width // BAND):
        tall[i * BAND : (i + 1) * BAND, :SETS] = wide[:, i * BAND : (i + 1) * BAND].T

    half_start = lax.rem(quarter // 2, 2) * 2 * width

    def pick(index, ranks_row, start, size):
        depth = 64
        positions = lax.broadcasted_iota(jnp.int32, (depth, 1), 0)

        def step(number, total):
            at = pl.ds(pl.multiple_of(start + number * depth, depth), depth)
            here = (positions + number * depth).astype(F32)
            root = tall[at, 4 + index : 5 + index]
            return total + jnp.sum(jnp.where(ranks_row == here, root, 0.0), axis=0, keepdims=True)

        return lax.fori_loop(0, size // depth, step, jnp.zeros((1, size), F32))

    group = quarter // 2
    half_ranks = jnp.concatenate(
        [tables[2 * group, 0:1], tables[2 * group + 1, 0:1]], axis=1
    )
    half_picked = pick(0, half_ranks, half_start, 2 * width)
    all_picked = pick(1, wide[1:2, :], 0, 4 * width)
    both = jnp.concatenate(
        [jnp.concatenate([half_picked, half_picked], axis=1), all_picked]
        + [jnp.zeros((6, 4 * width), F32)], axis=0
    )
    for i in range(4 * width // BAND):
        picked[i * BAND : (i + 1) * BAND, :SETS] = both[:, i * BAND : (i + 1) * BAND].T

    def weigh(index, start, size, own_start):
        depth = 64
        own = tables[quarter, 2 + index : 3 + index]
        own_place = own_start + lax.broadcasted_iota(jnp.int32, (1, width), 1)
        positions = lax.broadcasted_iota(jnp.int32, (depth, 1), 0)

        def step(number, total):
            at = pl.ds(pl.multiple_of(start + number * depth, depth), depth)
            within = pl.ds(pl.multiple_of(number * depth, depth), depth)
            pole = tall[at, 2 + index : 3 + index]
            living = tall[at, 6 + index : 7 + index] == 0.0
            root = picked[within, index : index + 1]
            between = jnp.where(positions + number * depth == own_place, 1.0, jnp.abs(pole - own))
            logs = jnp.log(jnp.abs(root - own) / between)
            return total + jnp.sum(jnp.where(living, logs, 0.0), axis=0, keepdims=True)

        total = lax.fori_loop(0, size // depth, step, jnp.zeros((1, width), F32), unroll=2)
        alive = tables[quarter, 6 + index : 7 + index] == 0.0
        return jnp.where(alive, jnp.exp(0.5 * total), 0.0)

    weight_one = weigh(0, half_start, 2 * width, lax.rem(quarter, 2) * width)
    weight_two = weigh(1, 0, 4 * width, quarter * width)
    shared[quarter] = jnp.concatenate([weight_one, weight_two, jnp.zeros((6, width), F32)], axis=0)
    weight_copies = [
        remote(shared.at[quarter], shared.at[quarter], weight_send.at[i], weight_recv.at[i], device)
        for i, device in enumerate((near_id, far_id, across_id))
    ]
    for copy in weight_copies:
        copy.start()

    def level(index, start, size, store, blocks):
        depth = 128

        def column(kind, step):
            at = pl.ds(pl.multiple_of(start + step * depth, depth), depth)
            return tall[at, 2 * kind + index : 2 * kind + index + 1]

        for number, (block, within) in enumerate(blocks):
            root_block = tables[block, 4 + index : 5 + index]
            here = (within * width + lax.broadcasted_iota(jnp.int32, (1, width), 1)).astype(F32)

            def cauchy(step, carry):
                norms, dead = carry
                at = pl.ds(pl.multiple_of(step * depth, depth), depth)
                shift = pl.ds(pl.multiple_of(start + step * depth, depth), depth)
                weight = spread_weights[shift, index : index + 1]
                value = weight / (column(1, step) - root_block)
                store[number, at] = value
                norms = norms + jnp.sum(value * value, axis=0, keepdims=True)
                match = column(0, step) == here
                dead = dead + jnp.sum(
                    jnp.where(match, column(3, step), 0.0), axis=0, keepdims=True
                )
                return norms, dead

            zero = jnp.zeros((1, width), F32)
            norms, dead = lax.fori_loop(0, size // depth, cauchy, (zero, zero), unroll=2)
            inverse = 1.0 / jnp.sqrt(norms)

            def finish(step, carry):
                at = pl.ds(pl.multiple_of(step * depth, depth), depth)
                match = (column(0, step) == here).astype(F32)
                store[number, at] = jnp.where(dead > 0.0, match, store[number, at] * inverse)
                return carry

            lax.fori_loop(0, size // depth, finish, 0, unroll=2)

    @pl.when(has_prev)
    def _():
        for copy in to_next:
            copy.wait_recv()

    halo_scales = jnp.where(has_prev, scales_above[...], 0.0)
    count = own_scales.shape[1]

    def any_scale(window):
        if window < 0:
            return jnp.zeros((SETS, 1), F32)
        if window < above_windows:
            index = count - above_windows + window
            return halo_scales[:, index : index + 1]
        return own_scale(window)

    for block in range(above_windows + 1):
        turn(block, any_scale(block - 1), any_scale(block))
    for index in range(SETS):
        sweep(index, index, above_windows + index)
    for chunk in range(half):
        send_chunk(chunk)

    for copy in weight_copies:
        copy.wait_recv()
    for i in range(4):
        for j in range(width // BAND):
            spread_weights[i * width + j * BAND : i * width + (j + 1) * BAND, :SETS] = shared[
                i, :, j * BAND : (j + 1) * BAND
            ].T
    for group in range(2):
        level(
            0, group * 2 * width, 2 * width, mix_one.at[group],
            [(2 * group, 0), (2 * group + 1, 1)],
        )
    level(1, 0, 4 * width, mix_two, [(quarter, quarter), (near, near), (far, far)])

    for which, (other, kept) in enumerate(((near, 2), (far, 1))):
        for part, source in enumerate((quarter, other)):
            group = source // 2
            at = pl.ds(pl.multiple_of(lax.rem(source, 2) * width, width), width)
            left = jnp.concatenate([mix_one[group, 0, at], mix_one[group, 1, at]], axis=1)
            under = pl.ds(pl.multiple_of(group * 2 * width, width), 2 * width)
            for side, block in enumerate((0, kept)):
                span = (which, slice(part * width, (part + 1) * width), slice(side * width, (side + 1) * width))
                if which == 1 and part == 0 and side == 0:
                    plan_high[span] = plan_high[(0,) + span[1:]]
                    plan_low[span] = plan_low[(0,) + span[1:]]
                    continue
                high, low = halves(mix_two[block, under])
                value = dot3(left, high, low)
                high, low = halves(value)
                plan_high[span] = high
                plan_low[span] = low

    def merge(step, carry):
        pair = lax.rem(step + half // 2, chunks // 2)
        for which in range(2):
            chunk = 2 * pair + which
            gather_copy(chunk, near_id if which == 0 else far_id).wait_recv()
            span = pl.ds(pl.multiple_of(chunk * CHUNK, CHUNK), CHUNK)
            mine = ext[pl.ds(pl.multiple_of(ABOVE + chunk * CHUNK, CHUNK), CHUNK)]
            left = jnp.concatenate([mine, gathered[span]], axis=1)
            away = slice(width, 2 * width)
            partial[span] = dot3(left, plan_high[which, :, away], plan_low[which, :, away])
            reduce_copy(chunk, far_id if which == 0 else near_id).start()
            home = slice(0, width)
            out[span] = dot3(left, plan_high[which, :, home], plan_low[which, :, home])
        return carry

    lax.fori_loop(0, chunks // 2, merge, 0)

    def collect(step, carry):
        pair = lax.rem(step + half // 2, chunks // 2)
        for which in range(2):
            chunk = 2 * pair + which
            reduce_copy(chunk, far_id if which == 0 else near_id).wait_recv()
            span = pl.ds(pl.multiple_of(chunk * CHUNK, CHUNK), CHUNK)
            out[span] = out[span] + arrived[span]
        return carry

    lax.fori_loop(0, chunks // 2, collect, 0)

    for chunk in range(chunks):
        gather_copy(chunk, near_id if chunk % 2 == 0 else far_id).wait_send()
        reduce_copy(chunk, far_id if chunk % 2 == 0 else near_id).wait_send()
    for copy in table_copies + weight_copies:
        copy.wait_send()

    @pl.when(has_prev)
    def _():
        for copy in to_prev:
            copy.wait_send()

    @pl.when(has_next)
    def _():
        for copy in to_next:
            copy.wait_send()


def per_device(slab, ranks, poles, roots, flags, reflectors, reflector_scales):
    rows, width = slab.shape
    chunks = rows // CHUNK
    total = ABOVE + rows + BELOW
    anywhere = pl.BlockSpec(memory_space=pl.ANY)
    dma = pltpu.SemaphoreType.DMA
    operands = (slab, ranks, poles, roots, flags, reflectors, reflector_scales)
    held = [pltpu.with_memory_space_constraint(x, pltpu.HBM) for x in operands]
    return pl.pallas_call(
        kernel,
        out_shape=pltpu.VMEM((rows, width), F32),
        in_specs=[anywhere] * 7,
        out_specs=pl.BlockSpec(memory_space=pltpu.VMEM),
        scratch_shapes=[
            pltpu.VMEM((total, width), F32),
            pltpu.VMEM((SETS, total), F32),
            pltpu.VMEM(reflector_scales.shape, F32),
            pltpu.VMEM(reflector_scales.shape, F32),
            pltpu.VMEM((total, 128), F32),
            pltpu.VMEM((rows, width), F32),
            pltpu.VMEM((4, 8, width), F32),
            pltpu.VMEM((4 * width, 128), F32),
            pltpu.VMEM((8, 4 * width), F32),
            pltpu.VMEM((2, 2, width), jnp.int32),
            pltpu.VMEM((2, 2, width), F32),
            pltpu.VMEM((4 * width, 128), F32),
            pltpu.VMEM((4, 8, width), F32),
            pltpu.VMEM((4 * width, 128), F32),
            pltpu.VMEM((2, 2, 2 * width, width), F32),
            pltpu.VMEM((3, 4 * width, width), F32),
            pltpu.VMEM((2, 2 * width, 2 * width), BF16),
            pltpu.VMEM((2, 2 * width, 2 * width), BF16),
            pltpu.VMEM((rows, width), F32),
            pltpu.VMEM((rows, width), F32),
            dma((7,)), dma((5,)), dma((5,)), dma((3,)), dma((3,)), dma((3,)), dma((3,)),
            dma((chunks,)), dma((chunks,)), dma((chunks,)), dma((chunks,)),
        ],
        compiler_params=pltpu.CompilerParams(
            collective_id=0, has_side_effects=True, vmem_limit_bytes=48 * 1024 * 1024
        ),
    )(*held)


def solution(mesh):
    return jax.shard_map(
        per_device,
        mesh=mesh,
        in_specs=(
            P("row", "col"),
            P(None, "col"),
            P(None, "col"),
            P(None, "col"),
            P(None, "col"),
            P(None, "row"),
            P(None, "row"),
        ),
        out_specs=P("row", "col"),
        check_vma=False,
    )
```

```python
import functools

import jax
import jax.numpy as jnp
from jax import lax
from jax.experimental import pallas as pl
from jax.experimental.pallas import tpu as pltpu
from jax.sharding import PartitionSpec as P

BAND = 128
SETS = 8
BELOW = 128
CHUNK = 256
RAW = 2
MESH = pl.DeviceIdType.MESH
F32 = jnp.float32
BF16 = jnp.bfloat16


def set_offset(index):
    return 1 + (SETS - 1 - index) * (BAND - 2) // (SETS - 1)


def halves(value):
    high = value.astype(BF16)
    low = (value - high.astype(F32)).astype(BF16)
    return high, low


def dot(left, right):
    return jnp.dot(left, right, preferred_element_type=F32)


def dot3(left, right_high, right_low):
    high, low = halves(left)
    return dot(high, right_high) + (dot(high, right_low) + dot(low, right_high))


def kernel(
    slab, ranks, poles, roots, flags, reflectors, scales, out,
    ext, refl, scales_own, turned, gathered, tables, tall, wide,
    raw_ints, raw_floats, picked, shared, spread_weights, projections, above, fixes,
    mix_one, mix_two, plan_high, plan_low, partial, arrived,
    local_sems, halo_send, halo_recv, table_send, table_recv, fix_send, fix_recv,
    weight_send, weight_recv, gather_send, gather_recv, reduce_send, reduce_recv,
):
    rows = slab.shape[0]
    width = slab.shape[1]
    chunks = rows // CHUNK
    windows = rows // BAND
    row = lax.axis_index("row")
    row_size = lax.axis_size("row")
    col = lax.axis_index("col")
    quarter = lax.rem(col, 4)
    quad = col - quarter
    near = quarter + 1 - 2 * lax.rem(quarter, 2)
    far = lax.rem(quarter + 2, 4)
    across = 3 - quarter
    near_id = (row, quad + near)
    far_id = (row, quad + far)
    across_id = (row, quad + across)
    has_prev = row > 0
    has_next = row < row_size - 1
    prev_id = (lax.max(row - 1, 0), col)
    next_id = (lax.min(row + 1, row_size - 1), col)

    own_rows = pl.ds(0, rows)
    own_slab = pltpu.make_async_copy(slab, ext.at[own_rows], local_sems.at[0])
    own_refl = pltpu.make_async_copy(reflectors, refl.at[:, own_rows], local_sems.at[1])
    own_scale_copy = pltpu.make_async_copy(scales, scales_own, local_sems.at[2])
    small = [
        pltpu.make_async_copy(ranks, raw_ints.at[0], local_sems.at[3]),
        pltpu.make_async_copy(flags, raw_ints.at[1], local_sems.at[4]),
        pltpu.make_async_copy(poles, raw_floats.at[0], local_sems.at[5]),
        pltpu.make_async_copy(roots, raw_floats.at[1], local_sems.at[6]),
    ]
    for copy in small:
        copy.start()
    own_refl.start()
    own_scale_copy.start()
    own_slab.start()

    barrier = pltpu.get_barrier_semaphore()
    for partner in (near_id, far_id, across_id):
        pl.semaphore_signal(barrier, inc=1, device_id=partner, device_id_type=MESH)

    @pl.when(has_prev)
    def _():
        pl.semaphore_signal(barrier, inc=1, device_id=prev_id, device_id_type=MESH)

    @pl.when(has_next)
    def _():
        pl.semaphore_signal(barrier, inc=1, device_id=next_id, device_id_type=MESH)

    for copy in small:
        copy.wait()
    tables[quarter] = jnp.concatenate(
        [raw_ints[0].astype(F32), raw_floats[0], raw_floats[1], raw_ints[1].astype(F32)], axis=0
    )

    pl.semaphore_wait(
        barrier, 3 + jnp.where(has_prev, 1, 0) + jnp.where(has_next, 1, 0)
    )

    def remote(source, target, send, recv, device):
        return pltpu.make_async_remote_copy(
            src_ref=source, dst_ref=target, send_sem=send, recv_sem=recv,
            device_id=device, device_id_type=MESH,
        )

    to_prev = [
        remote(reflectors.at[:, pl.ds(0, BELOW)], refl.at[:, pl.ds(rows, BELOW)],
               halo_send.at[0], halo_recv.at[0], prev_id),
        remote(slab.at[pl.ds(0, BELOW)], ext.at[pl.ds(rows, BELOW)],
               halo_send.at[1], halo_recv.at[1], prev_id),
    ]
    per_chunk = CHUNK // BAND
    kept_first = (chunks - RAW) * per_chunk - 1
    last_window = (windows - 1 - kept_first) * SETS
    to_next = remote(projections.at[pl.ds(last_window, SETS)], above,
                     halo_send.at[2], halo_recv.at[2], next_id)

    table_copies = [
        remote(tables.at[quarter], tables.at[quarter], table_send.at[i], table_recv.at[i], device)
        for i, device in enumerate((near_id, far_id, across_id))
    ]
    for copy in table_copies:
        copy.start()

    def gather_copy(chunk, device):
        held = slab if isinstance(chunk, int) and chunk >= chunks - RAW else ext
        return remote(
            held.at[pl.ds(chunk * CHUNK, CHUNK)],
            gathered.at[pl.ds(chunk * CHUNK, CHUNK)],
            gather_send.at[chunk], gather_recv.at[chunk], device,
        )

    def reduce_copy(chunk, device):
        span = pl.ds(chunk * CHUNK, CHUNK)
        return remote(
            partial.at[span], arrived.at[span],
            reduce_send.at[chunk], reduce_recv.at[chunk], device,
        )

    def send_chunk(chunk):
        gather_copy(chunk, near_id if chunk % 2 == 0 else far_id).start()

    for chunk in range(chunks - RAW, chunks):
        send_chunk(chunk)

    @pl.when(has_prev)
    def _():
        for copy in to_prev:
            copy.start()

    @pl.when(jnp.logical_not(has_prev))
    def _():
        above[...] = jnp.zeros((SETS, width), F32)

    @pl.when(jnp.logical_not(has_next))
    def _():
        ext[pl.ds(rows, BELOW)] = jnp.zeros((BELOW, width), F32)
        refl[:, pl.ds(rows, BELOW)] = jnp.zeros((SETS, BELOW), F32)

    own_refl.wait()
    own_scale_copy.wait()

    def turn(block):
        span = slice(block * BAND, (block + 1) * BAND)
        turned[span, :SETS] = refl[:, span].T

    for block in range(windows):
        turn(block)

    place = lax.broadcasted_iota(jnp.int32, (BAND + 8, 1), 0)
    own_scales = scales_own[...]

    def sweep(index, number):
        offset = set_offset(index)
        base, shift = offset // 8 * 8, offset % 8
        inside = (place >= shift) & (place < BAND + shift)
        span = slice(number * BAND + base, number * BAND + base + BAND + 8)
        blade = jnp.where(inside, turned[span, index : index + 1], 0.0)
        panel = ext[span]
        projection = jnp.sum(blade * panel, axis=0, keepdims=True)
        projection = projection * own_scales[index : index + 1, number : number + 1]
        if number >= kept_first:
            at = (number - kept_first) * SETS + index
            projections[at : at + 1] = projection
        ext[span] = panel - blade * projection

    own_slab.wait()
    for index in range(SETS):
        for number in range(index, windows - 1):
            sweep(index, number)

    for copy in table_copies:
        copy.wait_recv()
    for i in range(4):
        wide[:, i * width : (i + 1) * width] = tables[i]
    for i in range(4 * width // BAND):
        tall[i * BAND : (i + 1) * BAND, :SETS] = wide[:, i * BAND : (i + 1) * BAND].T

    half_start = lax.rem(quarter // 2, 2) * 2 * width

    def fold(value):
        return jnp.sum(value.reshape(value.shape[0] // 8, 8, value.shape[1]), axis=0)

    def pick(index, ranks_row, start, size):
        depth = 64
        positions = lax.broadcasted_iota(jnp.int32, (depth, 1), 0)

        def step(number, total):
            at = pl.ds(pl.multiple_of(start + number * depth, depth), depth)
            here = (positions + number * depth).astype(F32)
            root = tall[at, 4 + index : 5 + index]
            return total + fold(jnp.where(ranks_row == here, root, 0.0))

        total = lax.fori_loop(0, size // depth, step, jnp.zeros((8, size), F32))
        return jnp.sum(total, axis=0, keepdims=True)

    group = quarter // 2
    half_ranks = jnp.concatenate(
        [tables[2 * group, 0:1], tables[2 * group + 1, 0:1]], axis=1
    )
    half_picked = pick(0, half_ranks, half_start, 2 * width)
    all_picked = pick(1, wide[1:2, :], 0, 4 * width)
    both = jnp.concatenate(
        [jnp.concatenate([half_picked, half_picked], axis=1), all_picked]
        + [jnp.zeros((6, 4 * width), F32)], axis=0
    )
    for i in range(4 * width // BAND):
        picked[i * BAND : (i + 1) * BAND, :SETS] = both[:, i * BAND : (i + 1) * BAND].T

    def weigh(index, start, size, own_start):
        depth = 64
        own = tables[quarter, 2 + index : 3 + index]
        own_place = own_start + lax.broadcasted_iota(jnp.int32, (1, width), 1)
        positions = lax.broadcasted_iota(jnp.int32, (depth, 1), 0)

        def step(number, total):
            at = pl.ds(pl.multiple_of(start + number * depth, depth), depth)
            within = pl.ds(pl.multiple_of(number * depth, depth), depth)
            pole = tall[at, 2 + index : 3 + index]
            living = tall[at, 6 + index : 7 + index] == 0.0
            root = picked[within, index : index + 1]
            between = jnp.where(positions + number * depth == own_place, 1.0, jnp.abs(pole - own))
            logs = jnp.log(jnp.abs(root - own) / between)
            return total + fold(jnp.where(living, logs, 0.0))

        total = lax.fori_loop(0, size // depth, step, jnp.zeros((8, width), F32), unroll=2)
        total = jnp.sum(total, axis=0, keepdims=True)
        alive = tables[quarter, 6 + index : 7 + index] == 0.0
        return jnp.where(alive, jnp.exp(0.5 * total), 0.0)

    @pl.when(has_next)
    def _():
        for copy in to_prev:
            copy.wait_recv()

    turn(windows)
    for index in range(SETS):
        sweep(index, windows - 1)

    @pl.when(has_next)
    def _():
        to_next.start()

    weight_one = weigh(0, half_start, 2 * width, lax.rem(quarter, 2) * width)
    weight_two = weigh(1, 0, 4 * width, quarter * width)
    shared[quarter] = jnp.concatenate([weight_one, weight_two, jnp.zeros((6, width), F32)], axis=0)
    weight_copies = [
        remote(shared.at[quarter], shared.at[quarter], weight_send.at[i], weight_recv.at[i], device)
        for i, device in enumerate((near_id, far_id, across_id))
    ]
    for copy in weight_copies:
        copy.start()
    for chunk in range(chunks - 2 * RAW, chunks - RAW):
        send_chunk(chunk)

    def level(index, start, size, store, blocks):
        depth = 128

        def column(kind, step):
            at = pl.ds(pl.multiple_of(start + step * depth, depth), depth)
            return tall[at, 2 * kind + index : 2 * kind + index + 1]

        for number, (block, within) in enumerate(blocks):
            root_block = tables[block, 4 + index : 5 + index]
            here = (within * width + lax.broadcasted_iota(jnp.int32, (1, width), 1)).astype(F32)

            def cauchy(step, carry):
                norms, dead = carry
                at = pl.ds(pl.multiple_of(step * depth, depth), depth)
                shift = pl.ds(pl.multiple_of(start + step * depth, depth), depth)
                weight = spread_weights[shift, index : index + 1]
                value = weight / (column(1, step) - root_block)
                store[number, at] = value
                norms = norms + jnp.sum(value * value, axis=0, keepdims=True)
                match = column(0, step) == here
                dead = dead + jnp.sum(
                    jnp.where(match, column(3, step), 0.0), axis=0, keepdims=True
                )
                return norms, dead

            zero = jnp.zeros((1, width), F32)
            norms, dead = lax.fori_loop(0, size // depth, cauchy, (zero, zero), unroll=2)
            inverse = 1.0 / jnp.sqrt(norms)

            def finish(step, carry):
                at = pl.ds(pl.multiple_of(step * depth, depth), depth)
                match = (column(0, step) == here).astype(F32)
                store[number, at] = jnp.where(dead > 0.0, match, store[number, at] * inverse)
                return carry

            lax.fori_loop(0, size // depth, finish, 0, unroll=2)

    fix_rows = (RAW // 2 * per_chunk + 2) * SETS
    fix_copies = [
        remote(projections.at[pl.ds(i * SETS, fix_rows)], fixes.at[i],
               fix_send.at[i], fix_recv.at[i], device)
        for i, device in enumerate((near_id, far_id))
    ]
    for copy in fix_copies:
        copy.start()

    @pl.when(has_prev)
    def _():
        to_next.wait_recv()

    head = lax.broadcasted_iota(jnp.int32, (BAND, 1), 0)
    for index in range(SETS):
        blade = jnp.where(head < set_offset(index), turned[:BAND, index : index + 1], 0.0)
        ext[:BAND] = ext[:BAND] - blade * above[index : index + 1]
        for number in range(index):
            sweep(index, number)
    for pair in reversed(range(chunks // 2 - RAW)):
        send_chunk(2 * pair)
        send_chunk(2 * pair + 1)

    for copy in weight_copies:
        copy.wait_recv()
    for i in range(4):
        for j in range(width // BAND):
            spread_weights[i * width + j * BAND : i * width + (j + 1) * BAND, :SETS] = shared[
                i, :, j * BAND : (j + 1) * BAND
            ].T
    for group in range(2):
        level(
            0, group * 2 * width, 2 * width, mix_one.at[group],
            [(2 * group, 0), (2 * group + 1, 1)],
        )
    level(1, 0, 4 * width, mix_two, [(quarter, quarter), (near, near), (far, far)])

    for which, (other, kept) in enumerate(((near, 2), (far, 1))):
        for part, source in enumerate((quarter, other)):
            group = source // 2
            at = pl.ds(pl.multiple_of(lax.rem(source, 2) * width, width), width)
            left = jnp.concatenate([mix_one[group, 0, at], mix_one[group, 1, at]], axis=1)
            under = pl.ds(pl.multiple_of(group * 2 * width, width), 2 * width)
            for side, block in enumerate((0, kept)):
                span = (which, slice(part * width, (part + 1) * width), slice(side * width, (side + 1) * width))
                if which == 1 and part == 0 and side == 0:
                    plan_high[span] = plan_high[(0,) + span[1:]]
                    plan_low[span] = plan_low[(0,) + span[1:]]
                    continue
                high, low = halves(mix_two[block, under])
                value = dot3(left, high, low)
                high, low = halves(value)
                plan_high[span] = high
                plan_low[span] = low

    for which, chunk in enumerate(range(chunks - RAW, chunks)):
        span = slice(chunk * CHUNK, (chunk + 1) * CHUNK)
        lines = chunk * CHUNK + lax.broadcasted_iota(jnp.int32, (SETS, CHUNK), 1)
        offsets = 1 + (SETS - 1 - lax.broadcasted_iota(jnp.int32, (SETS, CHUNK), 0)) * (
            (BAND - 2) // (SETS - 1)
        )
        blades = []
        for number in range(kept_first + which, kept_first + which + fix_rows // SETS):
            starts = offsets + number * BAND
            inside = (lines >= starts) & (lines < starts + BAND)
            blades.append(jnp.where(inside, refl[:, span], 0.0))
        fix_copies[which].wait_recv()
        high, low = halves(fixes[which])
        correction = dot3(jnp.concatenate(blades, axis=0).T, high, low)
        gather_copy(chunk, near_id if which == 0 else far_id).wait_recv()
        gathered[span] = gathered[span] - correction

    def merge(step, carry):
        pair = chunks // 2 - 1 - step
        for which in range(2):
            chunk = 2 * pair + which

            @pl.when(step > 0)
            def _():
                gather_copy(chunk, near_id if which == 0 else far_id).wait_recv()

            span = pl.ds(pl.multiple_of(chunk * CHUNK, CHUNK), CHUNK)
            mine = ext[span]
            left = jnp.concatenate([mine, gathered[span]], axis=1)
            away = slice(width, 2 * width)
            partial[span] = dot3(left, plan_high[which, :, away], plan_low[which, :, away])
            reduce_copy(chunk, far_id if which == 0 else near_id).start()
            home = slice(0, width)
            out[span] = dot3(left, plan_high[which, :, home], plan_low[which, :, home])
        return carry

    lax.fori_loop(0, chunks // 2, merge, 0)

    def collect(step, carry):
        pair = chunks // 2 - 1 - step
        for which in range(2):
            chunk = 2 * pair + which
            reduce_copy(chunk, far_id if which == 0 else near_id).wait_recv()
            span = pl.ds(pl.multiple_of(chunk * CHUNK, CHUNK), CHUNK)
            out[span] = out[span] + arrived[span]
        return carry

    lax.fori_loop(0, chunks // 2, collect, 0)

    for chunk in range(chunks):
        gather_copy(chunk, near_id if chunk % 2 == 0 else far_id).wait_send()
        reduce_copy(chunk, far_id if chunk % 2 == 0 else near_id).wait_send()
    for copy in table_copies + weight_copies + fix_copies:
        copy.wait_send()

    @pl.when(has_prev)
    def _():
        for copy in to_prev:
            copy.wait_send()

    @pl.when(has_next)
    def _():
        to_next.wait_send()


def per_device(slab, ranks, poles, roots, flags, reflectors, reflector_scales):
    rows, width = slab.shape
    chunks = rows // CHUNK
    total = rows + BELOW
    kept = (RAW * (CHUNK // BAND) + 1) * SETS
    fix_rows = (RAW // 2 * (CHUNK // BAND) + 2) * SETS
    anywhere = pl.BlockSpec(memory_space=pl.ANY)
    dma = pltpu.SemaphoreType.DMA
    operands = (slab, ranks, poles, roots, flags, reflectors, reflector_scales)
    held = [pltpu.with_memory_space_constraint(x, pltpu.HBM) for x in operands]
    return pl.pallas_call(
        kernel,
        out_shape=pltpu.VMEM((rows, width), F32),
        in_specs=[anywhere] * 7,
        out_specs=pl.BlockSpec(memory_space=pltpu.VMEM),
        scratch_shapes=[
            pltpu.VMEM((total, width), F32),
            pltpu.VMEM((SETS, total), F32),
            pltpu.VMEM(reflector_scales.shape, F32),
            pltpu.VMEM((total, 128), F32),
            pltpu.VMEM((rows, width), F32),
            pltpu.VMEM((4, 8, width), F32),
            pltpu.VMEM((4 * width, 128), F32),
            pltpu.VMEM((8, 4 * width), F32),
            pltpu.VMEM((2, 2, width), jnp.int32),
            pltpu.VMEM((2, 2, width), F32),
            pltpu.VMEM((4 * width, 128), F32),
            pltpu.VMEM((4, 8, width), F32),
            pltpu.VMEM((4 * width, 128), F32),
            pltpu.VMEM((kept, width), F32),
            pltpu.VMEM((SETS, width), F32),
            pltpu.VMEM((2, fix_rows, width), F32),
            pltpu.VMEM((2, 2, 2 * width, width), F32),
            pltpu.VMEM((3, 4 * width, width), F32),
            pltpu.VMEM((2, 2 * width, 2 * width), BF16),
            pltpu.VMEM((2, 2 * width, 2 * width), BF16),
            pltpu.VMEM((rows, width), F32),
            pltpu.VMEM((rows, width), F32),
            dma((7,)), dma((3,)), dma((3,)), dma((3,)), dma((3,)), dma((2,)), dma((2,)),
            dma((3,)), dma((3,)),
            dma((chunks,)), dma((chunks,)), dma((chunks,)), dma((chunks,)),
        ],
        compiler_params=pltpu.CompilerParams(
            collective_id=0, has_side_effects=True, vmem_limit_bytes=48 * 1024 * 1024
        ),
    )(*held)


def solution(mesh):
    return jax.shard_map(
        per_device,
        mesh=mesh,
        in_specs=(
            P("row", "col"),
            P(None, "col"),
            P(None, "col"),
            P(None, "col"),
            P(None, "col"),
            P(None, "row"),
            P(None, "row"),
        ),
        out_specs=P("row", "col"),
        check_vma=False,
    )
```

```python
import functools

import jax
import jax.numpy as jnp
from jax import lax
from jax.experimental import pallas as pl
from jax.experimental.pallas import tpu as pltpu
from jax.sharding import PartitionSpec as P

BAND = 128
SETS = 8
BELOW = 128
CHUNK = 256
PIECE = 128
RAW = 2
MESH = pl.DeviceIdType.MESH
F32 = jnp.float32
BF16 = jnp.bfloat16


def set_offset(index):
    return 1 + (SETS - 1 - index) * (BAND - 2) // (SETS - 1)


def halves(value):
    high = value.astype(BF16)
    low = (value - high.astype(F32)).astype(BF16)
    return high, low


def dot(left, right):
    return jnp.dot(left, right, preferred_element_type=F32)


def dot3(left, right_high, right_low):
    high, low = halves(left)
    return dot(high, right_high) + (dot(high, right_low) + dot(low, right_high))


def kernel(
    slab, ranks, poles, roots, flags, reflectors, scales, out,
    ext, refl, scales_own, turned, gathered, tables, tall, wide,
    raw_ints, raw_floats, picked, shared, spread_weights, projections, above, fixes,
    mix_one, mix_two, plan_high, plan_low, partial, arrived,
    local_sems, halo_send, halo_recv, table_send, table_recv, fix_send, fix_recv,
    weight_send, weight_recv, gather_send, gather_recv, reduce_send, reduce_recv, ready,
):
    rows = slab.shape[0]
    width = slab.shape[1]
    chunks = rows // CHUNK
    windows = rows // BAND
    row = lax.axis_index("row")
    row_size = lax.axis_size("row")
    col = lax.axis_index("col")
    quarter = lax.rem(col, 4)
    quad = col - quarter
    near = quarter + 1 - 2 * lax.rem(quarter, 2)
    far = lax.rem(quarter + 2, 4)
    across = 3 - quarter
    near_id = (row, quad + near)
    far_id = (row, quad + far)
    across_id = (row, quad + across)
    odd = lax.rem(row, 2) == 1
    even = jnp.logical_not(odd)
    has_prev = row > 0
    has_next = row < row_size - 1
    prev_id = (lax.max(row - 1, 0), col)
    next_id = (lax.min(row + 1, row_size - 1), col)

    barrier = pltpu.get_barrier_semaphore()
    for partner in (near_id, far_id, across_id):
        pl.semaphore_signal(barrier, inc=1, device_id=partner, device_id_type=MESH)

    @pl.when(odd & has_prev)
    def _():
        pl.semaphore_signal(barrier, inc=1, device_id=prev_id, device_id_type=MESH)

    @pl.when(odd & has_next)
    def _():
        pl.semaphore_signal(barrier, inc=1, device_id=next_id, device_id_type=MESH)

    own_rows = pl.ds(0, rows)
    own_slab = pltpu.make_async_copy(slab, ext.at[own_rows], local_sems.at[0])
    own_refl = pltpu.make_async_copy(reflectors, refl.at[:, own_rows], local_sems.at[1])
    own_scale_copy = pltpu.make_async_copy(scales, scales_own, local_sems.at[2])
    small = [
        pltpu.make_async_copy(ranks, raw_ints.at[0], local_sems.at[3]),
        pltpu.make_async_copy(flags, raw_ints.at[1], local_sems.at[4]),
        pltpu.make_async_copy(poles, raw_floats.at[0], local_sems.at[5]),
        pltpu.make_async_copy(roots, raw_floats.at[1], local_sems.at[6]),
    ]
    for copy in small:
        copy.start()
    own_refl.start()
    own_scale_copy.start()
    own_slab.start()

    for copy in small:
        copy.wait()
    tables[quarter] = jnp.concatenate(
        [raw_ints[0].astype(F32), raw_floats[0], raw_floats[1], raw_ints[1].astype(F32)], axis=0
    )

    pl.semaphore_wait(
        barrier, 3 + jnp.where(even & has_prev, 1, 0) + jnp.where(even & has_next, 1, 0)
    )

    def remote(source, target, send, recv, device):
        return pltpu.make_async_remote_copy(
            src_ref=source, dst_ref=target, send_sem=send, recv_sem=recv,
            device_id=device, device_id_type=MESH,
        )

    to_prev = [
        remote(reflectors.at[:, pl.ds(0, BELOW)], refl.at[:, pl.ds(rows, BELOW)],
               halo_send.at[0], halo_recv.at[0], prev_id),
        remote(slab.at[pl.ds(0, BELOW)], ext.at[pl.ds(rows, BELOW)],
               halo_send.at[1], halo_recv.at[1], prev_id),
    ]
    per_chunk = CHUNK // BAND
    kept_first = (chunks - RAW) * per_chunk - 1
    last_window = (windows - 1 - kept_first) * SETS
    to_next = remote(projections.at[pl.ds(last_window, SETS)], above,
                     halo_send.at[2], halo_recv.at[2], next_id)

    table_copies = [
        remote(tables.at[quarter], tables.at[quarter], table_send.at[i], table_recv.at[i], device)
        for i, device in enumerate((near_id, far_id, across_id))
    ]
    for copy in table_copies:
        copy.start()

    pieces = CHUNK // PIECE

    def gather_copy(chunk, part, device):
        held = slab if isinstance(chunk, int) and chunk >= chunks - RAW else ext
        span = pl.ds(chunk * CHUNK + part * PIECE, PIECE)
        number = chunk * pieces + part
        return remote(
            held.at[span], gathered.at[span],
            gather_send.at[number], gather_recv.at[number], device,
        )

    def reduce_copy(chunk, device):
        span = pl.ds(chunk * CHUNK, CHUNK)
        return remote(
            partial.at[span], arrived.at[span],
            reduce_send.at[chunk], reduce_recv.at[chunk], device,
        )

    def send_pair(pair, parts):
        for i in parts:
            gather_copy(2 * pair, i, near_id).start()
            gather_copy(2 * pair + 1, i, far_id).start()

    send_pair(chunks // 2 - 1, range(pieces))

    @pl.when(even & has_prev)
    def _():
        pl.semaphore_signal(ready.at[1], inc=1, device_id=prev_id, device_id_type=MESH)
        for copy in to_prev:
            copy.start()

    @pl.when(even & has_next)
    def _():
        pl.semaphore_signal(ready.at[0], inc=1, device_id=next_id, device_id_type=MESH)

    @pl.when(jnp.logical_not(has_prev))
    def _():
        above[...] = jnp.zeros((SETS, width), F32)

    @pl.when(jnp.logical_not(has_next))
    def _():
        ext[pl.ds(rows, BELOW)] = jnp.zeros((BELOW, width), F32)
        refl[:, pl.ds(rows, BELOW)] = jnp.zeros((SETS, BELOW), F32)

    own_refl.wait()
    own_scale_copy.wait()

    def turn(block):
        span = slice(block * BAND, (block + 1) * BAND)
        turned[span, :SETS] = refl[:, span].T

    for block in range(windows):
        turn(block)

    place = lax.broadcasted_iota(jnp.int32, (BAND + 8, 1), 0)
    own_scales = scales_own[...]

    def sweep(index, number):
        offset = set_offset(index)
        base, shift = offset // 8 * 8, offset % 8
        inside = (place >= shift) & (place < BAND + shift)
        span = slice(number * BAND + base, number * BAND + base + BAND + 8)
        blade = jnp.where(inside, turned[span, index : index + 1], 0.0)
        panel = ext[span]
        projection = jnp.sum(blade * panel, axis=0, keepdims=True)
        projection = projection * own_scales[index : index + 1, number : number + 1]
        if number >= kept_first:
            at = (number - kept_first) * SETS + index
            projections[at : at + 1] = projection
        ext[span] = panel - blade * projection

    own_slab.wait()
    for index in range(SETS):
        for number in range(index, windows - 1):
            sweep(index, number)
    send_pair(chunks // 2 - 2, range(pieces // 2))

    @pl.when(odd & has_prev)
    def _():
        pl.semaphore_wait(ready.at[0], 1)
        for copy in to_prev:
            copy.start()

    for copy in table_copies:
        copy.wait_recv()
    for i in range(4):
        wide[:, i * width : (i + 1) * width] = tables[i]
    for i in range(4 * width // BAND):
        tall[i * BAND : (i + 1) * BAND, :SETS] = wide[:, i * BAND : (i + 1) * BAND].T

    half_start = lax.rem(quarter // 2, 2) * 2 * width

    def fold(value):
        return jnp.sum(value.reshape(value.shape[0] // 8, 8, value.shape[1]), axis=0)

    def pick(index, ranks_row, start, size):
        depth = 64
        positions = lax.broadcasted_iota(jnp.int32, (depth, 1), 0)

        def step(number, total):
            at = pl.ds(pl.multiple_of(start + number * depth, depth), depth)
            here = (positions + number * depth).astype(F32)
            root = tall[at, 4 + index : 5 + index]
            return total + fold(jnp.where(ranks_row == here, root, 0.0))

        total = lax.fori_loop(0, size // depth, step, jnp.zeros((8, size), F32))
        return jnp.sum(total, axis=0, keepdims=True)

    group = quarter // 2
    half_ranks = jnp.concatenate(
        [tables[2 * group, 0:1], tables[2 * group + 1, 0:1]], axis=1
    )
    half_picked = pick(0, half_ranks, half_start, 2 * width)
    all_picked = pick(1, wide[1:2, :], 0, 4 * width)
    both = jnp.concatenate(
        [jnp.concatenate([half_picked, half_picked], axis=1), all_picked]
        + [jnp.zeros((6, 4 * width), F32)], axis=0
    )
    for i in range(4 * width // BAND):
        picked[i * BAND : (i + 1) * BAND, :SETS] = both[:, i * BAND : (i + 1) * BAND].T

    def weigh(index, start, size, own_start):
        depth = 64
        own = tables[quarter, 2 + index : 3 + index]
        own_place = own_start + lax.broadcasted_iota(jnp.int32, (1, width), 1)
        positions = lax.broadcasted_iota(jnp.int32, (depth, 1), 0)

        def step(number, total):
            at = pl.ds(pl.multiple_of(start + number * depth, depth), depth)
            within = pl.ds(pl.multiple_of(number * depth, depth), depth)
            pole = tall[at, 2 + index : 3 + index]
            living = tall[at, 6 + index : 7 + index] == 0.0
            root = picked[within, index : index + 1]
            between = jnp.where(positions + number * depth == own_place, 1.0, jnp.abs(pole - own))
            logs = jnp.log(jnp.abs(root - own) / between)
            return total + fold(jnp.where(living, logs, 0.0))

        total = lax.fori_loop(0, size // depth, step, jnp.zeros((8, width), F32), unroll=2)
        total = jnp.sum(total, axis=0, keepdims=True)
        alive = tables[quarter, 6 + index : 7 + index] == 0.0
        return jnp.where(alive, jnp.exp(0.5 * total), 0.0)

    weight_one = weigh(0, half_start, 2 * width, lax.rem(quarter, 2) * width)
    weight_two = weigh(1, 0, 4 * width, quarter * width)
    shared[quarter] = jnp.concatenate([weight_one, weight_two, jnp.zeros((6, width), F32)], axis=0)
    weight_copies = [
        remote(shared.at[quarter], shared.at[quarter], weight_send.at[i], weight_recv.at[i], device)
        for i, device in enumerate((near_id, far_id, across_id))
    ]
    for copy in weight_copies:
        copy.start()
    send_pair(chunks // 2 - 2, range(pieces // 2, pieces))

    def level(index, start, size, store, blocks):
        depth = 128

        def column(kind, step):
            at = pl.ds(pl.multiple_of(start + step * depth, depth), depth)
            return tall[at, 2 * kind + index : 2 * kind + index + 1]

        for number, (block, within) in enumerate(blocks):
            root_block = tables[block, 4 + index : 5 + index]
            here = (within * width + lax.broadcasted_iota(jnp.int32, (1, width), 1)).astype(F32)

            def cauchy(step, carry):
                norms, dead = carry
                at = pl.ds(pl.multiple_of(step * depth, depth), depth)
                shift = pl.ds(pl.multiple_of(start + step * depth, depth), depth)
                weight = spread_weights[shift, index : index + 1]
                value = weight / (column(1, step) - root_block)
                store[number, at] = value
                norms = norms + jnp.sum(value * value, axis=0, keepdims=True)
                match = column(0, step) == here
                dead = dead + jnp.sum(
                    jnp.where(match, column(3, step), 0.0), axis=0, keepdims=True
                )
                return norms, dead

            zero = jnp.zeros((1, width), F32)
            norms, dead = lax.fori_loop(0, size // depth, cauchy, (zero, zero), unroll=2)
            inverse = 1.0 / jnp.sqrt(norms)

            def finish(step, carry):
                at = pl.ds(pl.multiple_of(step * depth, depth), depth)
                match = (column(0, step) == here).astype(F32)
                store[number, at] = jnp.where(dead > 0.0, match, store[number, at] * inverse)
                return carry

            lax.fori_loop(0, size // depth, finish, 0, unroll=2)

    @pl.when(has_next)
    def _():
        for copy in to_prev:
            copy.wait_recv()

    turn(windows)
    for index in range(SETS):
        sweep(index, windows - 1)

    @pl.when(odd & has_next)
    def _():
        pl.semaphore_wait(ready.at[1], 1)

    @pl.when(has_next)
    def _():
        to_next.start()

    fix_rows = (per_chunk + 1) * SETS
    fix_copies = [
        remote(projections.at[pl.ds(i * per_chunk * SETS, fix_rows)],
               fixes.at[i, pl.ds(0, fix_rows)],
               fix_send.at[i], fix_recv.at[i], device)
        for i, device in enumerate((near_id, far_id))
    ]
    for copy in fix_copies:
        copy.start()

    @pl.when(has_prev)
    def _():
        to_next.wait_recv()

    head = lax.broadcasted_iota(jnp.int32, (BAND, 1), 0)
    for index in range(SETS):
        blade = jnp.where(head < set_offset(index), turned[:BAND, index : index + 1], 0.0)
        ext[:BAND] = ext[:BAND] - blade * above[index : index + 1]
        for number in range(index):
            sweep(index, number)
    for pair in reversed(range(chunks // 2 - RAW)):
        send_pair(pair, range(pieces))

    for copy in weight_copies:
        copy.wait_recv()
    for i in range(4):
        for j in range(width // BAND):
            spread_weights[i * width + j * BAND : i * width + (j + 1) * BAND, :SETS] = shared[
                i, :, j * BAND : (j + 1) * BAND
            ].T
    for group in range(2):
        level(
            0, group * 2 * width, 2 * width, mix_one.at[group],
            [(2 * group, 0), (2 * group + 1, 1)],
        )
    level(1, 0, 4 * width, mix_two, [(quarter, quarter), (near, near), (far, far)])

    for which, (other, kept) in enumerate(((near, 2), (far, 1))):
        for part, source in enumerate((quarter, other)):
            group = source // 2
            at = pl.ds(pl.multiple_of(lax.rem(source, 2) * width, width), width)
            left = jnp.concatenate([mix_one[group, 0, at], mix_one[group, 1, at]], axis=1)
            under = pl.ds(pl.multiple_of(group * 2 * width, width), 2 * width)
            for side, block in enumerate((0, kept)):
                span = (which, slice(part * width, (part + 1) * width), slice(side * width, (side + 1) * width))
                if which == 1 and part == 0 and side == 0:
                    plan_high[span] = plan_high[(0,) + span[1:]]
                    plan_low[span] = plan_low[(0,) + span[1:]]
                    continue
                high, low = halves(mix_two[block, under])
                value = dot3(left, high, low)
                high, low = halves(value)
                plan_high[span] = high
                plan_low[span] = low

    for which, chunk in enumerate(range(chunks - RAW, chunks)):
        span = slice(chunk * CHUNK, (chunk + 1) * CHUNK)
        lines = chunk * CHUNK + lax.broadcasted_iota(jnp.int32, (SETS, CHUNK), 1)
        offsets = 1 + (SETS - 1 - lax.broadcasted_iota(jnp.int32, (SETS, CHUNK), 0)) * (
            (BAND - 2) // (SETS - 1)
        )
        blades = []
        for number in range(per_chunk + 1):
            starts = offsets + (kept_first + which * per_chunk + number) * BAND
            inside = (lines >= starts) & (lines < starts + BAND)
            blades.append(jnp.where(inside, refl[:, span], 0.0))
        spare = fixes.shape[1] - fix_rows
        blades.append(jnp.zeros((spare, CHUNK), F32))
        fix_copies[which].wait_recv()
        reached = jnp.concatenate([fixes[which, :fix_rows], jnp.zeros((spare, width), F32)], axis=0)
        high, low = halves(reached)
        correction = dot3(jnp.concatenate(blades, axis=0).T, high, low)
        for i in range(pieces):
            gather_copy(chunk, i, near_id if which == 0 else far_id).wait_recv()
        gathered[span] = gathered[span] - correction

    def merge(step, carry):
        pair = chunks // 2 - 1 - step
        for which in range(2):
            chunk = 2 * pair + which

            @pl.when(step > 0)
            def _():
                for i in range(pieces):
                    gather_copy(chunk, i, near_id if which == 0 else far_id).wait_recv()

            span = pl.ds(pl.multiple_of(chunk * CHUNK, CHUNK), CHUNK)
            mine = ext[span]
            left = jnp.concatenate([mine, gathered[span]], axis=1)
            away = slice(width, 2 * width)
            partial[span] = dot3(left, plan_high[which, :, away], plan_low[which, :, away])
            reduce_copy(chunk, far_id if which == 0 else near_id).start()
            home = slice(0, width)
            out[span] = dot3(left, plan_high[which, :, home], plan_low[which, :, home])
        return carry

    lax.fori_loop(0, chunks // 2, merge, 0)

    for chunk in range(chunks):
        for i in range(pieces):
            gather_copy(chunk, i, near_id if chunk % 2 == 0 else far_id).wait_send()
    for copy in table_copies + weight_copies + fix_copies:
        copy.wait_send()

    @pl.when(has_prev)
    def _():
        for copy in to_prev:
            copy.wait_send()

    @pl.when(has_next)
    def _():
        to_next.wait_send()

    def collect(step, carry):
        pair = chunks // 2 - 1 - step
        for which in range(2):
            chunk = 2 * pair + which
            copy = reduce_copy(chunk, far_id if which == 0 else near_id)
            copy.wait_recv()
            span = pl.ds(pl.multiple_of(chunk * CHUNK, CHUNK), CHUNK)
            out[span] = out[span] + arrived[span]
            copy.wait_send()
        return carry

    lax.fori_loop(0, chunks // 2, collect, 0)


def per_device(slab, ranks, poles, roots, flags, reflectors, reflector_scales):
    rows, width = slab.shape
    chunks = rows // CHUNK
    total = rows + BELOW
    kept = (RAW * (CHUNK // BAND) + 1) * SETS
    fix_rows = (CHUNK // BAND + 2) * SETS
    anywhere = pl.BlockSpec(memory_space=pl.ANY)
    dma = pltpu.SemaphoreType.DMA
    operands = (slab, ranks, poles, roots, flags, reflectors, reflector_scales)
    held = [pltpu.with_memory_space_constraint(x, pltpu.HBM) for x in operands]
    return pl.pallas_call(
        kernel,
        out_shape=pltpu.VMEM((rows, width), F32),
        in_specs=[anywhere] * 7,
        out_specs=pl.BlockSpec(memory_space=pltpu.VMEM),
        scratch_shapes=[
            pltpu.VMEM((total, width), F32),
            pltpu.VMEM((SETS, total), F32),
            pltpu.VMEM(reflector_scales.shape, F32),
            pltpu.VMEM((total, 128), F32),
            pltpu.VMEM((rows, width), F32),
            pltpu.VMEM((4, 8, width), F32),
            pltpu.VMEM((4 * width, 128), F32),
            pltpu.VMEM((8, 4 * width), F32),
            pltpu.VMEM((2, 2, width), jnp.int32),
            pltpu.VMEM((2, 2, width), F32),
            pltpu.VMEM((4 * width, 128), F32),
            pltpu.VMEM((4, 8, width), F32),
            pltpu.VMEM((4 * width, 128), F32),
            pltpu.VMEM((kept, width), F32),
            pltpu.VMEM((SETS, width), F32),
            pltpu.VMEM((2, fix_rows, width), F32),
            pltpu.VMEM((2, 2, 2 * width, width), F32),
            pltpu.VMEM((3, 4 * width, width), F32),
            pltpu.VMEM((2, 2 * width, 2 * width), BF16),
            pltpu.VMEM((2, 2 * width, 2 * width), BF16),
            pltpu.VMEM((rows, width), F32),
            pltpu.VMEM((rows, width), F32),
            dma((7,)), dma((3,)), dma((3,)), dma((3,)), dma((3,)), dma((2,)), dma((2,)),
            dma((3,)), dma((3,)),
            dma((rows // PIECE,)), dma((rows // PIECE,)), dma((chunks,)), dma((chunks,)),
            pltpu.SemaphoreType.REGULAR((2,)),
        ],
        compiler_params=pltpu.CompilerParams(
            collective_id=0, has_side_effects=True, vmem_limit_bytes=48 * 1024 * 1024
        ),
    )(*held)


def solution(mesh):
    return jax.shard_map(
        per_device,
        mesh=mesh,
        in_specs=(
            P("row", "col"),
            P(None, "col"),
            P(None, "col"),
            P(None, "col"),
            P(None, "col"),
            P(None, "row"),
            P(None, "row"),
        ),
        out_specs=P("row", "col"),
        check_vma=False,
    )
```

```python
import functools

import jax
import jax.numpy as jnp
from jax import lax
from jax.experimental import pallas as pl
from jax.experimental.pallas import tpu as pltpu
from jax.sharding import PartitionSpec as P

BAND = 128
SETS = 8
BELOW = 128
CHUNK = 256
PIECE = 128
RAW = 2
MESH = pl.DeviceIdType.MESH
F32 = jnp.float32
BF16 = jnp.bfloat16


def set_offset(index):
    return 1 + (SETS - 1 - index) * (BAND - 2) // (SETS - 1)


def halves(value):
    high = value.astype(BF16)
    low = (value - high.astype(F32)).astype(BF16)
    return high, low


def dot(left, right):
    return jnp.dot(left, right, preferred_element_type=F32)


def dot3(left, right_high, right_low):
    high, low = halves(left)
    return dot(high, right_high) + (dot(high, right_low) + dot(low, right_high))


def kernel(
    slab, ranks, poles, roots, flags, reflectors, scales, out,
    ext, refl, scales_own, turned, gathered, tables, tall, wide,
    raw_ints, raw_floats, weight_columns, shared, spread_weights, projections, above, fixes,
    mix_one, mix_two, plan_high, plan_low, partial, arrived,
    local_sems, halo_send, halo_recv, table_send, table_recv, fix_send, fix_recv,
    weight_send, weight_recv, gather_send, gather_recv, reduce_send, reduce_recv, ready,
):
    rows = slab.shape[0]
    width = slab.shape[1]
    chunks = rows // CHUNK
    windows = rows // BAND
    row = lax.axis_index("row")
    row_size = lax.axis_size("row")
    col = lax.axis_index("col")
    quarter = lax.rem(col, 4)
    quad = col - quarter
    near = quarter + 1 - 2 * lax.rem(quarter, 2)
    far = lax.rem(quarter + 2, 4)
    across = 3 - quarter
    near_id = (row, quad + near)
    far_id = (row, quad + far)
    across_id = (row, quad + across)
    odd = lax.rem(row, 2) == 1
    even = jnp.logical_not(odd)
    has_prev = row > 0
    has_next = row < row_size - 1
    prev_id = (lax.max(row - 1, 0), col)
    next_id = (lax.min(row + 1, row_size - 1), col)

    barrier = pltpu.get_barrier_semaphore()
    for partner in (near_id, far_id, across_id):
        pl.semaphore_signal(barrier, inc=1, device_id=partner, device_id_type=MESH)

    @pl.when(odd & has_prev)
    def _():
        pl.semaphore_signal(barrier, inc=1, device_id=prev_id, device_id_type=MESH)

    @pl.when(odd & has_next)
    def _():
        pl.semaphore_signal(barrier, inc=1, device_id=next_id, device_id_type=MESH)

    own_rows = pl.ds(0, rows)
    own_slab = pltpu.make_async_copy(slab, ext.at[own_rows], local_sems.at[0])
    own_refl = pltpu.make_async_copy(reflectors, refl.at[:, own_rows], local_sems.at[1])
    own_scale_copy = pltpu.make_async_copy(scales, scales_own, local_sems.at[2])
    small = [
        pltpu.make_async_copy(ranks, raw_ints.at[0], local_sems.at[3]),
        pltpu.make_async_copy(flags, raw_ints.at[1], local_sems.at[4]),
        pltpu.make_async_copy(poles, raw_floats.at[0], local_sems.at[5]),
        pltpu.make_async_copy(roots, raw_floats.at[1], local_sems.at[6]),
    ]
    for copy in small:
        copy.start()
    own_refl.start()
    own_scale_copy.start()
    own_slab.start()

    for copy in small:
        copy.wait()
    tables[quarter] = jnp.concatenate(
        [raw_ints[0].astype(F32), raw_floats[0], raw_floats[1], raw_ints[1].astype(F32)], axis=0
    )

    pl.semaphore_wait(
        barrier, 3 + jnp.where(even & has_prev, 1, 0) + jnp.where(even & has_next, 1, 0)
    )

    def remote(source, target, send, recv, device):
        return pltpu.make_async_remote_copy(
            src_ref=source, dst_ref=target, send_sem=send, recv_sem=recv,
            device_id=device, device_id_type=MESH,
        )

    to_prev = [
        remote(reflectors.at[:, pl.ds(0, BELOW)], refl.at[:, pl.ds(rows, BELOW)],
               halo_send.at[0], halo_recv.at[0], prev_id),
        remote(slab.at[pl.ds(0, BELOW)], ext.at[pl.ds(rows, BELOW)],
               halo_send.at[1], halo_recv.at[1], prev_id),
    ]
    per_chunk = CHUNK // BAND
    kept_first = (chunks - RAW) * per_chunk - 1
    last_window = (windows - 1 - kept_first) * SETS
    to_next = remote(projections.at[pl.ds(last_window, SETS)], above,
                     halo_send.at[2], halo_recv.at[2], next_id)

    table_copies = [
        remote(tables.at[quarter], tables.at[quarter], table_send.at[i], table_recv.at[i], device)
        for i, device in enumerate((near_id, far_id, across_id))
    ]
    for copy in table_copies:
        copy.start()

    pieces = CHUNK // PIECE

    def gather_copy(chunk, part, device):
        held = slab if isinstance(chunk, int) and chunk >= chunks - RAW else ext
        span = pl.ds(chunk * CHUNK + part * PIECE, PIECE)
        number = chunk * pieces + part
        return remote(
            held.at[span], gathered.at[span],
            gather_send.at[number], gather_recv.at[number], device,
        )

    def reduce_copy(chunk, device):
        span = pl.ds(chunk * CHUNK, CHUNK)
        return remote(
            partial.at[span], arrived.at[span],
            reduce_send.at[chunk], reduce_recv.at[chunk], device,
        )

    def send_pair(pair, parts):
        for i in parts:
            gather_copy(2 * pair, i, near_id).start()
            gather_copy(2 * pair + 1, i, far_id).start()

    send_pair(chunks // 2 - 1, range(pieces))

    @pl.when(even & has_prev)
    def _():
        pl.semaphore_signal(ready.at[1], inc=1, device_id=prev_id, device_id_type=MESH)
        for copy in to_prev:
            copy.start()

    @pl.when(even & has_next)
    def _():
        pl.semaphore_signal(ready.at[0], inc=1, device_id=next_id, device_id_type=MESH)

    @pl.when(jnp.logical_not(has_prev))
    def _():
        above[...] = jnp.zeros((SETS, width), F32)

    @pl.when(jnp.logical_not(has_next))
    def _():
        ext[pl.ds(rows, BELOW)] = jnp.zeros((BELOW, width), F32)
        refl[:, pl.ds(rows, BELOW)] = jnp.zeros((SETS, BELOW), F32)

    own_refl.wait()
    own_scale_copy.wait()

    def turn(block):
        span = slice(block * BAND, (block + 1) * BAND)
        turned[span, :SETS] = refl[:, span].T

    for block in range(windows):
        turn(block)

    place = lax.broadcasted_iota(jnp.int32, (BAND + 8, 1), 0)
    own_scales = scales_own[...]

    def sweep(index, number):
        offset = set_offset(index)
        base, shift = offset // 8 * 8, offset % 8
        inside = (place >= shift) & (place < BAND + shift)
        span = slice(number * BAND + base, number * BAND + base + BAND + 8)
        blade = jnp.where(inside, turned[span, index : index + 1], 0.0)
        panel = ext[span]
        projection = jnp.sum(blade * panel, axis=0, keepdims=True)
        projection = projection * own_scales[index : index + 1, number : number + 1]
        if number >= kept_first:
            at = (number - kept_first) * SETS + index
            projections[at : at + 1] = projection
        ext[span] = panel - blade * projection

    own_slab.wait()
    for index in range(SETS):
        for number in range(index, windows - 1):
            sweep(index, number)
    send_pair(chunks // 2 - 2, range(pieces // 2))

    @pl.when(odd & has_prev)
    def _():
        pl.semaphore_wait(ready.at[0], 1)
        for copy in to_prev:
            copy.start()

    for copy in table_copies:
        copy.wait_recv()
    for i in range(4):
        span = slice(i * width, (i + 1) * width)
        wide[:6, span] = tables[i, :6]
        wide[6:, span] = jnp.where(tables[i, 6:] != 0.0, tables[i, :2], -1.0)
    for i in range(4 * width // BAND):
        tall[i * BAND : (i + 1) * BAND, :SETS] = wide[:, i * BAND : (i + 1) * BAND].T

    half_start = lax.rem(quarter // 2, 2) * 2 * width

    def fold(value):
        return jnp.sum(value.reshape(value.shape[0] // 8, 8, value.shape[1]), axis=0)

    def pick(index, ranks_row, start, size):
        depth = 64
        positions = lax.broadcasted_iota(jnp.int32, (depth, 1), 0)

        def step(number, total):
            at = pl.ds(pl.multiple_of(start + number * depth, depth), depth)
            here = (positions + number * depth).astype(F32)
            root = tall[at, 4 + index : 5 + index]
            return total + fold(jnp.where(ranks_row == here, root, 0.0))

        total = lax.fori_loop(0, size // depth, step, jnp.zeros((8, size), F32))
        return jnp.sum(total, axis=0, keepdims=True)

    group = quarter // 2
    half_ranks = jnp.concatenate(
        [tables[2 * group, 0:1], tables[2 * group + 1, 0:1]], axis=1
    )
    half_picked = pick(0, half_ranks, half_start, 2 * width)
    all_picked = pick(1, wide[1:2, :], 0, 4 * width)
    def weigh(index, pole, root, dead_rank, own_start):
        depth = 64
        lanes = lax.broadcasted_iota(jnp.int32, (1, BAND), 1)
        places = lax.broadcasted_iota(jnp.int32, (depth, 1), 0)
        living = dead_rank < 0.0

        def step(number, carry):
            at = pl.ds(pl.multiple_of(quarter * width + number * depth, depth), depth)
            own = tall[at, 2 + index : 3 + index]
            own_place = own_start + number * depth + places
            total = jnp.zeros((depth, BAND), F32)
            for tile in range(pole.shape[1] // BAND):
                span = slice(tile * BAND, (tile + 1) * BAND)
                apart = jnp.abs(pole[:, span] - own)
                between = jnp.where(lanes + tile * BAND == own_place, 1.0, apart)
                logs = jnp.log(jnp.abs(root[:, span] - own) / between)
                total = total + jnp.where(living[:, span], logs, 0.0)
            alive = tall[at, 6 + index : 7 + index] < 0.0
            weight = jnp.exp(0.5 * jnp.sum(total, axis=1, keepdims=True))
            within = pl.ds(pl.multiple_of(number * depth, depth), depth)
            weight_columns[within, index : index + 1] = jnp.where(alive, weight, 0.0)
            return carry

        lax.fori_loop(0, width // depth, step, 0)

    def half_row(kind):
        return jnp.concatenate(
            [wide_part(2 * group)[kind : kind + 1], wide_part(2 * group + 1)[kind : kind + 1]], axis=1
        )

    def wide_part(number):
        return wide[:, pl.ds(pl.multiple_of(number * width, width), width)]

    weight_columns[...] = jnp.zeros(weight_columns.shape, F32)
    weigh(0, half_row(2), half_picked, half_row(6), lax.rem(quarter, 2) * width)
    weigh(1, wide[3:4, :], all_picked, wide[7:8, :], quarter * width)
    for i in range(width // BAND):
        span = slice(i * BAND, (i + 1) * BAND)
        shared[quarter, :, span] = weight_columns[span, :SETS].T[:2]
    weight_copies = [
        remote(shared.at[quarter], shared.at[quarter], weight_send.at[i], weight_recv.at[i], device)
        for i, device in enumerate((near_id, far_id, across_id))
    ]
    for copy in weight_copies:
        copy.start()
    send_pair(chunks // 2 - 2, range(pieces // 2, pieces))

    def level(index, start, size, store, blocks):
        depth = 64
        roots_of = [tables[block, 4 + index : 5 + index] for block, _ in blocks]
        ranks_of = [
            (within * width + lax.broadcasted_iota(jnp.int32, (1, width), 1)).astype(F32)
            for _, within in blocks
        ]

        def cauchy(step, carry):
            at = pl.ds(pl.multiple_of(step * depth, depth), depth)
            shift = pl.ds(pl.multiple_of(start + step * depth, depth), depth)
            weight = spread_weights[shift, index : index + 1]
            pole = tall[shift, 2 + index : 3 + index]
            dead_rank = tall[shift, 6 + index : 7 + index]
            sums = []
            for number in range(len(blocks)):
                norms, dead = carry[number]
                value = weight / (pole - roots_of[number])
                store[number, at] = value
                norms = norms + fold(value * value)
                dead = dead + fold(jnp.where(dead_rank == ranks_of[number], 1.0, 0.0))
                sums.append((norms, dead))
            return tuple(sums)

        zero = jnp.zeros((8, width), F32)
        sums = lax.fori_loop(0, size // depth, cauchy, ((zero, zero),) * len(blocks))
        scales_of = [
            jnp.where(
                jnp.sum(dead, axis=0, keepdims=True) > 0.0, 0.0,
                1.0 / jnp.sqrt(jnp.sum(norms, axis=0, keepdims=True)),
            )
            for norms, dead in sums
        ]

        def finish(step, carry):
            at = pl.ds(pl.multiple_of(step * depth, depth), depth)
            shift = pl.ds(pl.multiple_of(start + step * depth, depth), depth)
            dead_rank = tall[shift, 6 + index : 7 + index]
            for number in range(len(blocks)):
                store[number, at] = jnp.where(
                    dead_rank == ranks_of[number], 1.0, store[number, at] * scales_of[number]
                )
            return carry

        lax.fori_loop(0, size // depth, finish, 0)

    @pl.when(has_next)
    def _():
        for copy in to_prev:
            copy.wait_recv()

    turn(windows)
    for index in range(SETS):
        sweep(index, windows - 1)

    @pl.when(odd & has_next)
    def _():
        pl.semaphore_wait(ready.at[1], 1)

    @pl.when(has_next)
    def _():
        to_next.start()

    fix_rows = (per_chunk + 1) * SETS
    fix_copies = [
        remote(projections.at[pl.ds(i * per_chunk * SETS, fix_rows)],
               fixes.at[i, pl.ds(0, fix_rows)],
               fix_send.at[i], fix_recv.at[i], device)
        for i, device in enumerate((near_id, far_id))
    ]
    for copy in fix_copies:
        copy.start()

    @pl.when(has_prev)
    def _():
        to_next.wait_recv()

    head = lax.broadcasted_iota(jnp.int32, (BAND, 1), 0)
    for index in range(SETS):
        blade = jnp.where(head < set_offset(index), turned[:BAND, index : index + 1], 0.0)
        ext[:BAND] = ext[:BAND] - blade * above[index : index + 1]
        for number in range(index):
            sweep(index, number)
    for pair in reversed(range(chunks // 2 - RAW)):
        send_pair(pair, range(pieces))

    for copy in weight_copies:
        copy.wait_recv()
    for i in range(4):
        for j in range(width // BAND):
            weights = shared[i, :, j * BAND : (j + 1) * BAND]
            padded = jnp.concatenate([weights, jnp.zeros((6, BAND), F32)], axis=0)
            spread_weights[i * width + j * BAND : i * width + (j + 1) * BAND, :SETS] = padded.T
    for group in range(2):
        level(
            0, group * 2 * width, 2 * width, mix_one.at[group],
            [(2 * group, 0), (2 * group + 1, 1)],
        )
    level(1, 0, 4 * width, mix_two, [(quarter, quarter), (near, near), (far, far)])

    for which, (other, kept) in enumerate(((near, 2), (far, 1))):
        for part, source in enumerate((quarter, other)):
            group = source // 2
            at = pl.ds(pl.multiple_of(lax.rem(source, 2) * width, width), width)
            left = jnp.concatenate([mix_one[group, 0, at], mix_one[group, 1, at]], axis=1)
            under = pl.ds(pl.multiple_of(group * 2 * width, width), 2 * width)
            for side, block in enumerate((0, kept)):
                span = (which, slice(part * width, (part + 1) * width), slice(side * width, (side + 1) * width))
                if which == 1 and part == 0 and side == 0:
                    plan_high[span] = plan_high[(0,) + span[1:]]
                    plan_low[span] = plan_low[(0,) + span[1:]]
                    continue
                high, low = halves(mix_two[block, under])
                value = dot3(left, high, low)
                high, low = halves(value)
                plan_high[span] = high
                plan_low[span] = low

    for which, chunk in enumerate(range(chunks - RAW, chunks)):
        span = slice(chunk * CHUNK, (chunk + 1) * CHUNK)
        lines = chunk * CHUNK + lax.broadcasted_iota(jnp.int32, (SETS, CHUNK), 1)
        offsets = 1 + (SETS - 1 - lax.broadcasted_iota(jnp.int32, (SETS, CHUNK), 0)) * (
            (BAND - 2) // (SETS - 1)
        )
        blades = []
        for number in range(per_chunk + 1):
            starts = offsets + (kept_first + which * per_chunk + number) * BAND
            inside = (lines >= starts) & (lines < starts + BAND)
            blades.append(jnp.where(inside, refl[:, span], 0.0))
        spare = fixes.shape[1] - fix_rows
        blades.append(jnp.zeros((spare, CHUNK), F32))
        fix_copies[which].wait_recv()
        reached = jnp.concatenate([fixes[which, :fix_rows], jnp.zeros((spare, width), F32)], axis=0)
        high, low = halves(reached)
        correction = dot3(jnp.concatenate(blades, axis=0).T, high, low)
        for i in range(pieces):
            gather_copy(chunk, i, near_id if which == 0 else far_id).wait_recv()
        gathered[span] = gathered[span] - correction

    def merge(step, carry):
        pair = chunks // 2 - 1 - step
        for which in range(2):
            chunk = 2 * pair + which

            @pl.when(step > 0)
            def _():
                for i in range(pieces):
                    gather_copy(chunk, i, near_id if which == 0 else far_id).wait_recv()

            span = pl.ds(pl.multiple_of(chunk * CHUNK, CHUNK), CHUNK)
            mine = ext[span]
            left = jnp.concatenate([mine, gathered[span]], axis=1)
            away = slice(width, 2 * width)
            partial[span] = dot3(left, plan_high[which, :, away], plan_low[which, :, away])
            reduce_copy(chunk, far_id if which == 0 else near_id).start()
            home = slice(0, width)
            out[span] = dot3(left, plan_high[which, :, home], plan_low[which, :, home])
        return carry

    lax.fori_loop(0, chunks // 2, merge, 0)

    for chunk in range(chunks):
        for i in range(pieces):
            gather_copy(chunk, i, near_id if chunk % 2 == 0 else far_id).wait_send()
    for copy in table_copies + weight_copies + fix_copies:
        copy.wait_send()

    @pl.when(has_prev)
    def _():
        for copy in to_prev:
            copy.wait_send()

    @pl.when(has_next)
    def _():
        to_next.wait_send()

    def collect(step, carry):
        pair = chunks // 2 - 1 - step
        for which in range(2):
            chunk = 2 * pair + which
            copy = reduce_copy(chunk, far_id if which == 0 else near_id)
            copy.wait_recv()
            span = pl.ds(pl.multiple_of(chunk * CHUNK, CHUNK), CHUNK)
            out[span] = out[span] + arrived[span]
            copy.wait_send()
        return carry

    lax.fori_loop(0, chunks // 2, collect, 0)


def per_device(slab, ranks, poles, roots, flags, reflectors, reflector_scales):
    rows, width = slab.shape
    chunks = rows // CHUNK
    total = rows + BELOW
    kept = (RAW * (CHUNK // BAND) + 1) * SETS
    fix_rows = (CHUNK // BAND + 2) * SETS
    anywhere = pl.BlockSpec(memory_space=pl.ANY)
    dma = pltpu.SemaphoreType.DMA
    operands = (slab, ranks, poles, roots, flags, reflectors, reflector_scales)
    held = [pltpu.with_memory_space_constraint(x, pltpu.HBM) for x in operands]
    return pl.pallas_call(
        kernel,
        out_shape=pltpu.VMEM((rows, width), F32),
        in_specs=[anywhere] * 7,
        out_specs=pl.BlockSpec(memory_space=pltpu.VMEM),
        scratch_shapes=[
            pltpu.VMEM((total, width), F32),
            pltpu.VMEM((SETS, total), F32),
            pltpu.VMEM(reflector_scales.shape, F32),
            pltpu.VMEM((total, 128), F32),
            pltpu.VMEM((rows, width), F32),
            pltpu.VMEM((4, 8, width), F32),
            pltpu.VMEM((4 * width, 128), F32),
            pltpu.VMEM((8, 4 * width), F32),
            pltpu.VMEM((2, 2, width), jnp.int32),
            pltpu.VMEM((2, 2, width), F32),
            pltpu.VMEM((width, 128), F32),
            pltpu.VMEM((4, 2, width), F32),
            pltpu.VMEM((4 * width, 128), F32),
            pltpu.VMEM((kept, width), F32),
            pltpu.VMEM((SETS, width), F32),
            pltpu.VMEM((2, fix_rows, width), F32),
            pltpu.VMEM((2, 2, 2 * width, width), F32),
            pltpu.VMEM((3, 4 * width, width), F32),
            pltpu.VMEM((2, 2 * width, 2 * width), BF16),
            pltpu.VMEM((2, 2 * width, 2 * width), BF16),
            pltpu.VMEM((rows, width), F32),
            pltpu.VMEM((rows, width), F32),
            dma((7,)), dma((3,)), dma((3,)), dma((3,)), dma((3,)), dma((2,)), dma((2,)),
            dma((3,)), dma((3,)),
            dma((rows // PIECE,)), dma((rows // PIECE,)), dma((chunks,)), dma((chunks,)),
            pltpu.SemaphoreType.REGULAR((2,)),
        ],
        compiler_params=pltpu.CompilerParams(
            collective_id=0, has_side_effects=True, vmem_limit_bytes=48 * 1024 * 1024
        ),
    )(*held)


def solution(mesh):
    return jax.shard_map(
        per_device,
        mesh=mesh,
        in_specs=(
            P("row", "col"),
            P(None, "col"),
            P(None, "col"),
            P(None, "col"),
            P(None, "col"),
            P(None, "row"),
            P(None, "row"),
        ),
        out_specs=P("row", "col"),
        check_vma=False,
    )
```

```python
import functools

import jax
import jax.numpy as jnp
from jax import lax
from jax.experimental import pallas as pl
from jax.experimental.pallas import tpu as pltpu
from jax.sharding import PartitionSpec as P

BAND = 128
SETS = 8
BELOW = 128
CHUNK = 256
PIECE = 128
MESH = pl.DeviceIdType.MESH
F32 = jnp.float32
BF16 = jnp.bfloat16


def set_offset(index):
    return 1 + (SETS - 1 - index) * (BAND - 2) // (SETS - 1)


def halves(value):
    high = value.astype(BF16)
    low = (value - high.astype(F32)).astype(BF16)
    return high, low


def dot(left, right):
    return jnp.dot(left, right, preferred_element_type=F32)


def dot3(left, right_high, right_low):
    high, low = halves(left)
    return dot(high, right_high) + (dot(high, right_low) + dot(low, right_high))


def kernel(
    slab, ranks, poles, roots, flags, reflectors, scales, out,
    ext, refl, scales_own, turned, gathered, tables, tall, wide,
    raw_ints, raw_floats, weight_columns, shared, spread_weights, projections, above, fixes,
    mix_one, mix_two, plan_high, plan_low, partial, arrived,
    local_sems, halo_send, halo_recv, table_send, table_recv, fix_send, fix_recv,
    weight_send, weight_recv, gather_send, gather_recv, reduce_send, reduce_recv, ready,
):
    rows = slab.shape[0]
    width = slab.shape[1]
    chunks = rows // CHUNK
    windows = rows // BAND
    row = lax.axis_index("row")
    row_size = lax.axis_size("row")
    col = lax.axis_index("col")
    quarter = lax.rem(col, 4)
    quad = col - quarter
    near = quarter + 1 - 2 * lax.rem(quarter, 2)
    far = lax.rem(quarter + 2, 4)
    across = 3 - quarter
    near_id = (row, quad + near)
    far_id = (row, quad + far)
    across_id = (row, quad + across)
    odd = lax.rem(row, 2) == 1
    even = jnp.logical_not(odd)
    has_prev = row > 0
    has_next = row < row_size - 1
    prev_id = (lax.max(row - 1, 0), col)
    next_id = (lax.min(row + 1, row_size - 1), col)

    barrier = pltpu.get_barrier_semaphore()
    for partner in (near_id, far_id, across_id):
        pl.semaphore_signal(barrier, inc=1, device_id=partner, device_id_type=MESH)

    @pl.when(odd & has_prev)
    def _():
        pl.semaphore_signal(barrier, inc=1, device_id=prev_id, device_id_type=MESH)

    @pl.when(odd & has_next)
    def _():
        pl.semaphore_signal(barrier, inc=1, device_id=next_id, device_id_type=MESH)

    own_rows = pl.ds(0, rows)
    own_slab = pltpu.make_async_copy(slab, ext.at[own_rows], local_sems.at[0])
    own_refl = pltpu.make_async_copy(reflectors, refl.at[:, own_rows], local_sems.at[1])
    own_scale_copy = pltpu.make_async_copy(scales, scales_own, local_sems.at[2])
    small = [
        pltpu.make_async_copy(ranks, raw_ints.at[0], local_sems.at[3]),
        pltpu.make_async_copy(flags, raw_ints.at[1], local_sems.at[4]),
        pltpu.make_async_copy(poles, raw_floats.at[0], local_sems.at[5]),
        pltpu.make_async_copy(roots, raw_floats.at[1], local_sems.at[6]),
    ]
    for copy in small:
        copy.start()
    own_refl.start()
    own_scale_copy.start()
    own_slab.start()

    for copy in small:
        copy.wait()
    tables[quarter] = jnp.concatenate(
        [raw_ints[0].astype(F32), raw_floats[0], raw_floats[1], raw_ints[1].astype(F32)], axis=0
    )

    pl.semaphore_wait(
        barrier, 3 + jnp.where(even & has_prev, 1, 0) + jnp.where(even & has_next, 1, 0)
    )

    def remote(source, target, send, recv, device):
        return pltpu.make_async_remote_copy(
            src_ref=source, dst_ref=target, send_sem=send, recv_sem=recv,
            device_id=device, device_id_type=MESH,
        )

    to_prev = [
        remote(reflectors.at[:, pl.ds(0, BELOW)], refl.at[:, pl.ds(rows, BELOW)],
               halo_send.at[0], halo_recv.at[0], prev_id),
        remote(slab.at[pl.ds(0, BELOW)], ext.at[pl.ds(rows, BELOW)],
               halo_send.at[1], halo_recv.at[1], prev_id),
    ]
    raw_start = (chunks - 1) * CHUNK - PIECE
    kept_first = raw_start // BAND - 1
    last_window = (windows - 1 - kept_first) * SETS
    to_next = remote(projections.at[pl.ds(last_window, SETS)], above,
                     halo_send.at[2], halo_recv.at[2], next_id)

    table_copies = [
        remote(tables.at[quarter], tables.at[quarter], table_send.at[i], table_recv.at[i], device)
        for i, device in enumerate((near_id, far_id, across_id))
    ]
    for copy in table_copies:
        copy.start()

    pieces = CHUNK // PIECE

    def gather_copy(chunk, part, device, held=ext):
        span = pl.ds(chunk * CHUNK + part * PIECE, PIECE)
        number = chunk * pieces + part
        return remote(
            held.at[span], gathered.at[span],
            gather_send.at[number], gather_recv.at[number], device,
        )

    def reduce_copy(chunk, device):
        span = pl.ds(chunk * CHUNK, CHUNK)
        return remote(
            partial.at[span], arrived.at[span],
            reduce_send.at[chunk], reduce_recv.at[chunk], device,
        )

    def send_pair(pair, parts):
        for i in parts:
            gather_copy(2 * pair, i, near_id).start()
            gather_copy(2 * pair + 1, i, far_id).start()

    raw_copies = [
        gather_copy(chunks - 2, 1, near_id, slab), gather_copy(chunks - 1, 0, far_id, slab)
    ]
    for copy in raw_copies:
        copy.start()

    @pl.when(even & has_prev)
    def _():
        pl.semaphore_signal(ready.at[1], inc=1, device_id=prev_id, device_id_type=MESH)
        for copy in to_prev:
            copy.start()

    @pl.when(even & has_next)
    def _():
        pl.semaphore_signal(ready.at[0], inc=1, device_id=next_id, device_id_type=MESH)

    @pl.when(jnp.logical_not(has_prev))
    def _():
        above[...] = jnp.zeros((SETS, width), F32)

    @pl.when(jnp.logical_not(has_next))
    def _():
        ext[pl.ds(rows, BELOW)] = jnp.zeros((BELOW, width), F32)
        refl[:, pl.ds(rows, BELOW)] = jnp.zeros((SETS, BELOW), F32)

    own_refl.wait()
    own_scale_copy.wait()

    def turn(block):
        span = slice(block * BAND, (block + 1) * BAND)
        turned[span, :SETS] = refl[:, span].T

    for block in range(windows):
        turn(block)

    place = lax.broadcasted_iota(jnp.int32, (BAND + 8, 1), 0)
    own_scales = scales_own[...]

    def sweep(index, number):
        offset = set_offset(index)
        base, shift = offset // 8 * 8, offset % 8
        inside = (place >= shift) & (place < BAND + shift)
        span = slice(number * BAND + base, number * BAND + base + BAND + 8)
        blade = jnp.where(inside, turned[span, index : index + 1], 0.0)
        panel = ext[span]
        projection = jnp.sum(blade * panel, axis=0, keepdims=True)
        projection = projection * own_scales[index : index + 1, number : number + 1]
        if number >= kept_first:
            at = (number - kept_first) * SETS + index
            projections[at : at + 1] = projection
        ext[span] = panel - blade * projection

    own_slab.wait()
    early = ((chunks - 3) * CHUNK + PIECE) // BAND
    for index in range(SETS):
        for number in range(index, early):
            sweep(index, number)
    send_pair(chunks // 2 - 2, range(1))
    for index in range(SETS):
        for number in range(early, windows - 1):
            sweep(index, number)
    send_pair(chunks // 2 - 2, range(1, pieces))

    @pl.when(odd & has_prev)
    def _():
        pl.semaphore_wait(ready.at[0], 1)
        for copy in to_prev:
            copy.start()

    for copy in table_copies:
        copy.wait_recv()
    for i in range(4):
        span = slice(i * width, (i + 1) * width)
        wide[:6, span] = tables[i, :6]
        wide[6:, span] = jnp.where(tables[i, 6:] != 0.0, tables[i, :2], -1.0)
    for i in range(4 * width // BAND):
        tall[i * BAND : (i + 1) * BAND, :SETS] = wide[:, i * BAND : (i + 1) * BAND].T

    half_start = lax.rem(quarter // 2, 2) * 2 * width

    def fold(value):
        return jnp.sum(value.reshape(value.shape[0] // 8, 8, value.shape[1]), axis=0)

    def pick(index, ranks_row, start, size):
        depth = 64
        positions = lax.broadcasted_iota(jnp.int32, (depth, 1), 0)

        def step(number, total):
            at = pl.ds(pl.multiple_of(start + number * depth, depth), depth)
            here = (positions + number * depth).astype(F32)
            root = tall[at, 4 + index : 5 + index]
            return total + fold(jnp.where(ranks_row == here, root, 0.0))

        total = lax.fori_loop(0, size // depth, step, jnp.zeros((8, size), F32))
        return jnp.sum(total, axis=0, keepdims=True)

    group = quarter // 2
    half_ranks = jnp.concatenate(
        [tables[2 * group, 0:1], tables[2 * group + 1, 0:1]], axis=1
    )
    half_picked = pick(0, half_ranks, half_start, 2 * width)
    all_picked = pick(1, wide[1:2, :], 0, 4 * width)
    def weigh(index, pole, root, dead_rank, own_start):
        depth = 64
        lanes = lax.broadcasted_iota(jnp.int32, (1, BAND), 1)
        places = lax.broadcasted_iota(jnp.int32, (depth, 1), 0)
        living = dead_rank < 0.0

        def step(number, carry):
            at = pl.ds(pl.multiple_of(quarter * width + number * depth, depth), depth)
            own = tall[at, 2 + index : 3 + index]
            own_place = own_start + number * depth + places
            total = jnp.zeros((depth, BAND), F32)
            for tile in range(pole.shape[1] // BAND):
                span = slice(tile * BAND, (tile + 1) * BAND)
                apart = jnp.abs(pole[:, span] - own)
                between = jnp.where(lanes + tile * BAND == own_place, 1.0, apart)
                logs = jnp.log(jnp.abs(root[:, span] - own) / between)
                total = total + jnp.where(living[:, span], logs, 0.0)
            alive = tall[at, 6 + index : 7 + index] < 0.0
            weight = jnp.exp(0.5 * jnp.sum(total, axis=1, keepdims=True))
            within = pl.ds(pl.multiple_of(number * depth, depth), depth)
            weight_columns[within, index : index + 1] = jnp.where(alive, weight, 0.0)
            return carry

        lax.fori_loop(0, width // depth, step, 0)

    def half_row(kind):
        return jnp.concatenate(
            [wide_part(2 * group)[kind : kind + 1], wide_part(2 * group + 1)[kind : kind + 1]], axis=1
        )

    def wide_part(number):
        return wide[:, pl.ds(pl.multiple_of(number * width, width), width)]

    weight_columns[...] = jnp.zeros(weight_columns.shape, F32)
    weigh(0, half_row(2), half_picked, half_row(6), lax.rem(quarter, 2) * width)
    weigh(1, wide[3:4, :], all_picked, wide[7:8, :], quarter * width)
    for i in range(width // BAND):
        span = slice(i * BAND, (i + 1) * BAND)
        shared[quarter, :, span] = weight_columns[span, :SETS].T[:2]
    weight_copies = [
        remote(shared.at[quarter], shared.at[quarter], weight_send.at[i], weight_recv.at[i], device)
        for i, device in enumerate((near_id, far_id, across_id))
    ]
    for copy in weight_copies:
        copy.start()
    fix_rows = (PIECE // BAND + 1) * SETS
    fix_copies = [
        remote(projections.at[pl.ds(i * SETS, fix_rows)], fixes.at[i],
               fix_send.at[i], fix_recv.at[i], device)
        for i, device in enumerate((near_id, far_id))
    ]
    for copy in fix_copies:
        copy.start()
    gather_copy(chunks - 2, 0, near_id).start()

    def level(index, start, size, store, blocks):
        depth = 64
        roots_of = [tables[block, 4 + index : 5 + index] for block, _ in blocks]
        ranks_of = [
            (within * width + lax.broadcasted_iota(jnp.int32, (1, width), 1)).astype(F32)
            for _, within in blocks
        ]

        def cauchy(step, carry):
            at = pl.ds(pl.multiple_of(step * depth, depth), depth)
            shift = pl.ds(pl.multiple_of(start + step * depth, depth), depth)
            weight = spread_weights[shift, index : index + 1]
            pole = tall[shift, 2 + index : 3 + index]
            dead_rank = tall[shift, 6 + index : 7 + index]
            sums = []
            for number in range(len(blocks)):
                norms, dead = carry[number]
                value = weight / (pole - roots_of[number])
                store[number, at] = value
                norms = norms + fold(value * value)
                dead = dead + fold(jnp.where(dead_rank == ranks_of[number], 1.0, 0.0))
                sums.append((norms, dead))
            return tuple(sums)

        zero = jnp.zeros((8, width), F32)
        sums = lax.fori_loop(0, size // depth, cauchy, ((zero, zero),) * len(blocks))
        scales_of = [
            jnp.where(
                jnp.sum(dead, axis=0, keepdims=True) > 0.0, 0.0,
                1.0 / jnp.sqrt(jnp.sum(norms, axis=0, keepdims=True)),
            )
            for norms, dead in sums
        ]

        def finish(step, carry):
            at = pl.ds(pl.multiple_of(step * depth, depth), depth)
            shift = pl.ds(pl.multiple_of(start + step * depth, depth), depth)
            dead_rank = tall[shift, 6 + index : 7 + index]
            for number in range(len(blocks)):
                store[number, at] = jnp.where(
                    dead_rank == ranks_of[number], 1.0, store[number, at] * scales_of[number]
                )
            return carry

        lax.fori_loop(0, size // depth, finish, 0)

    @pl.when(has_next)
    def _():
        for copy in to_prev:
            copy.wait_recv()

    turn(windows)
    for index in range(SETS):
        sweep(index, windows - 1)

    @pl.when(odd & has_next)
    def _():
        pl.semaphore_wait(ready.at[1], 1)

    gather_copy(chunks - 1, 1, far_id).start()

    @pl.when(has_next)
    def _():
        to_next.start()

    @pl.when(has_prev)
    def _():
        to_next.wait_recv()

    head = lax.broadcasted_iota(jnp.int32, (BAND, 1), 0)
    for index in range(SETS):
        blade = jnp.where(head < set_offset(index), turned[:BAND, index : index + 1], 0.0)
        ext[:BAND] = ext[:BAND] - blade * above[index : index + 1]
        for number in range(index):
            sweep(index, number)
    for pair in reversed(range(chunks // 2 - 2)):
        send_pair(pair, range(pieces))

    for copy in weight_copies:
        copy.wait_recv()
    for i in range(4):
        for j in range(width // BAND):
            weights = shared[i, :, j * BAND : (j + 1) * BAND]
            padded = jnp.concatenate([weights, jnp.zeros((6, BAND), F32)], axis=0)
            spread_weights[i * width + j * BAND : i * width + (j + 1) * BAND, :SETS] = padded.T
    for group in range(2):
        level(
            0, group * 2 * width, 2 * width, mix_one.at[group],
            [(2 * group, 0), (2 * group + 1, 1)],
        )
    level(1, 0, 4 * width, mix_two, [(quarter, quarter), (near, near), (far, far)])

    for which, (other, kept) in enumerate(((near, 2), (far, 1))):
        for part, source in enumerate((quarter, other)):
            group = source // 2
            at = pl.ds(pl.multiple_of(lax.rem(source, 2) * width, width), width)
            left = jnp.concatenate([mix_one[group, 0, at], mix_one[group, 1, at]], axis=1)
            under = pl.ds(pl.multiple_of(group * 2 * width, width), 2 * width)
            for side, block in enumerate((0, kept)):
                span = (which, slice(part * width, (part + 1) * width), slice(side * width, (side + 1) * width))
                if which == 1 and part == 0 and side == 0:
                    plan_high[span] = plan_high[(0,) + span[1:]]
                    plan_low[span] = plan_low[(0,) + span[1:]]
                    continue
                high, low = halves(mix_two[block, under])
                value = dot3(left, high, low)
                high, low = halves(value)
                plan_high[span] = high
                plan_low[span] = low

    for which in range(2):
        start = raw_start + which * PIECE
        span = slice(start, start + PIECE)
        lines = start + lax.broadcasted_iota(jnp.int32, (SETS, PIECE), 1)
        offsets = 1 + (SETS - 1 - lax.broadcasted_iota(jnp.int32, (SETS, PIECE), 0)) * (
            (BAND - 2) // (SETS - 1)
        )
        blades = []
        for number in range(fix_rows // SETS):
            starts = offsets + (kept_first + which + number) * BAND
            inside = (lines >= starts) & (lines < starts + BAND)
            blades.append(jnp.where(inside, refl[:, span], 0.0))
        fix_copies[which].wait_recv()
        high, low = halves(fixes[which])
        correction = dot3(jnp.concatenate(blades, axis=0).T, high, low)
        raw_copies[which].wait_recv()
        gathered[span] = gathered[span] - correction

    def pair_of(step):
        return jnp.where(step < 2, chunks // 2 - 2 + step, chunks // 2 - 1 - step)

    def merge(step, carry):
        pair = pair_of(step)
        for which in range(2):
            chunk = 2 * pair + which

            gather_copy(chunk, which, near_id if which == 0 else far_id).wait_recv()

            @pl.when(step != 1)
            def _():
                gather_copy(chunk, 1 - which, near_id if which == 0 else far_id).wait_recv()

            span = pl.ds(pl.multiple_of(chunk * CHUNK, CHUNK), CHUNK)
            mine = ext[span]
            left = jnp.concatenate([mine, gathered[span]], axis=1)
            away = slice(width, 2 * width)
            partial[span] = dot3(left, plan_high[which, :, away], plan_low[which, :, away])
            reduce_copy(chunk, far_id if which == 0 else near_id).start()
            home = slice(0, width)
            out[span] = dot3(left, plan_high[which, :, home], plan_low[which, :, home])
        return carry

    lax.fori_loop(0, chunks // 2, merge, 0)

    for chunk in range(chunks):
        for i in range(pieces):
            gather_copy(chunk, i, near_id if chunk % 2 == 0 else far_id).wait_send()
    for copy in table_copies + weight_copies + fix_copies:
        copy.wait_send()

    @pl.when(has_prev)
    def _():
        for copy in to_prev:
            copy.wait_send()

    @pl.when(has_next)
    def _():
        to_next.wait_send()

    def collect(step, carry):
        pair = pair_of(step)
        for which in range(2):
            chunk = 2 * pair + which
            copy = reduce_copy(chunk, far_id if which == 0 else near_id)
            copy.wait_recv()
            span = pl.ds(pl.multiple_of(chunk * CHUNK, CHUNK), CHUNK)
            out[span] = out[span] + arrived[span]
            copy.wait_send()
        return carry

    lax.fori_loop(0, chunks // 2, collect, 0)


def per_device(slab, ranks, poles, roots, flags, reflectors, reflector_scales):
    rows, width = slab.shape
    chunks = rows // CHUNK
    total = rows + BELOW
    kept = (CHUNK // BAND + 2) * SETS
    fix_rows = (PIECE // BAND + 1) * SETS
    anywhere = pl.BlockSpec(memory_space=pl.ANY)
    dma = pltpu.SemaphoreType.DMA
    operands = (slab, ranks, poles, roots, flags, reflectors, reflector_scales)
    held = [pltpu.with_memory_space_constraint(x, pltpu.HBM) for x in operands]
    return pl.pallas_call(
        kernel,
        out_shape=pltpu.VMEM((rows, width), F32),
        in_specs=[anywhere] * 7,
        out_specs=pl.BlockSpec(memory_space=pltpu.VMEM),
        scratch_shapes=[
            pltpu.VMEM((total, width), F32),
            pltpu.VMEM((SETS, total), F32),
            pltpu.VMEM(reflector_scales.shape, F32),
            pltpu.VMEM((total, 128), F32),
            pltpu.VMEM((rows, width), F32),
            pltpu.VMEM((4, 8, width), F32),
            pltpu.VMEM((4 * width, 128), F32),
            pltpu.VMEM((8, 4 * width), F32),
            pltpu.VMEM((2, 2, width), jnp.int32),
            pltpu.VMEM((2, 2, width), F32),
            pltpu.VMEM((width, 128), F32),
            pltpu.VMEM((4, 2, width), F32),
            pltpu.VMEM((4 * width, 128), F32),
            pltpu.VMEM((kept, width), F32),
            pltpu.VMEM((SETS, width), F32),
            pltpu.VMEM((2, fix_rows, width), F32),
            pltpu.VMEM((2, 2, 2 * width, width), F32),
            pltpu.VMEM((3, 4 * width, width), F32),
            pltpu.VMEM((2, 2 * width, 2 * width), BF16),
            pltpu.VMEM((2, 2 * width, 2 * width), BF16),
            pltpu.VMEM((rows, width), F32),
            pltpu.VMEM((rows, width), F32),
            dma((7,)), dma((3,)), dma((3,)), dma((3,)), dma((3,)), dma((2,)), dma((2,)),
            dma((3,)), dma((3,)),
            dma((rows // PIECE,)), dma((rows // PIECE,)), dma((chunks,)), dma((chunks,)),
            pltpu.SemaphoreType.REGULAR((2,)),
        ],
        compiler_params=pltpu.CompilerParams(
            collective_id=0, has_side_effects=True, vmem_limit_bytes=48 * 1024 * 1024
        ),
    )(*held)


def solution(mesh):
    return jax.shard_map(
        per_device,
        mesh=mesh,
        in_specs=(
            P("row", "col"),
            P(None, "col"),
            P(None, "col"),
            P(None, "col"),
            P(None, "col"),
            P(None, "row"),
            P(None, "row"),
        ),
        out_specs=P("row", "col"),
        check_vma=False,
    )
```

```python
import functools

import jax
import jax.numpy as jnp
from jax import lax
from jax.experimental import pallas as pl
from jax.experimental.pallas import tpu as pltpu
from jax.sharding import PartitionSpec as P

BAND = 128
SETS = 8
BELOW = 128
CHUNK = 256
PIECE = 128
MESH = pl.DeviceIdType.MESH
F32 = jnp.float32
BF16 = jnp.bfloat16


def set_offset(index):
    return 1 + (SETS - 1 - index) * (BAND - 2) // (SETS - 1)


def halves(value):
    high = value.astype(BF16)
    low = (value - high.astype(F32)).astype(BF16)
    return high, low


def dot(left, right):
    return jnp.dot(left, right, preferred_element_type=F32)


def dot3(left, right_high, right_low):
    high, low = halves(left)
    return dot(high, right_high) + (dot(high, right_low) + dot(low, right_high))


def kernel(
    slab, ranks, poles, roots, flags, reflectors, scales, out,
    ext, refl, scales_own, turned, gathered, tables, tall, wide,
    raw_ints, raw_floats, weights, projections, above, fixes,
    mix_one, mix_two, plan_high, plan_low, partial, arrived,
    local_sems, halo_send, halo_recv, table_send, table_recv, fix_send, fix_recv,
    gather_send, gather_recv, reduce_send, reduce_recv, ready,
):
    rows = slab.shape[0]
    width = slab.shape[1]
    chunks = rows // CHUNK
    windows = rows // BAND
    row = lax.axis_index("row")
    row_size = lax.axis_size("row")
    col = lax.axis_index("col")
    quarter = lax.rem(col, 4)
    quad = col - quarter
    near = quarter + 1 - 2 * lax.rem(quarter, 2)
    far = lax.rem(quarter + 2, 4)
    across = 3 - quarter
    near_id = (row, quad + near)
    far_id = (row, quad + far)
    across_id = (row, quad + across)
    odd = lax.rem(row, 2) == 1
    even = jnp.logical_not(odd)
    has_prev = row > 0
    has_next = row < row_size - 1
    prev_id = (lax.max(row - 1, 0), col)
    next_id = (lax.min(row + 1, row_size - 1), col)

    barrier = pltpu.get_barrier_semaphore()
    for partner in (near_id, far_id, across_id):
        pl.semaphore_signal(barrier, inc=1, device_id=partner, device_id_type=MESH)

    @pl.when(odd & has_prev)
    def _():
        pl.semaphore_signal(barrier, inc=1, device_id=prev_id, device_id_type=MESH)

    @pl.when(odd & has_next)
    def _():
        pl.semaphore_signal(barrier, inc=1, device_id=next_id, device_id_type=MESH)

    own_rows = pl.ds(0, rows)
    own_slab = pltpu.make_async_copy(slab, ext.at[own_rows], local_sems.at[0])
    own_refl = pltpu.make_async_copy(reflectors, refl.at[:, own_rows], local_sems.at[1])
    own_scale_copy = pltpu.make_async_copy(scales, scales_own, local_sems.at[2])
    small = [
        pltpu.make_async_copy(ranks, raw_ints.at[0], local_sems.at[3]),
        pltpu.make_async_copy(flags, raw_ints.at[1], local_sems.at[4]),
        pltpu.make_async_copy(poles, raw_floats.at[0], local_sems.at[5]),
        pltpu.make_async_copy(roots, raw_floats.at[1], local_sems.at[6]),
    ]
    for copy in small:
        copy.start()
    own_refl.start()
    own_scale_copy.start()
    own_slab.start()

    for copy in small:
        copy.wait()
    tables[quarter] = jnp.concatenate(
        [raw_ints[0].astype(F32), raw_floats[0], raw_floats[1], raw_ints[1].astype(F32)], axis=0
    )

    pl.semaphore_wait(
        barrier, 3 + jnp.where(even & has_prev, 1, 0) + jnp.where(even & has_next, 1, 0)
    )

    def remote(source, target, send, recv, device):
        return pltpu.make_async_remote_copy(
            src_ref=source, dst_ref=target, send_sem=send, recv_sem=recv,
            device_id=device, device_id_type=MESH,
        )

    to_prev = [
        remote(reflectors.at[:, pl.ds(0, BELOW)], refl.at[:, pl.ds(rows, BELOW)],
               halo_send.at[0], halo_recv.at[0], prev_id),
        remote(slab.at[pl.ds(0, BELOW)], ext.at[pl.ds(rows, BELOW)],
               halo_send.at[1], halo_recv.at[1], prev_id),
    ]
    raw_start = (chunks - 1) * CHUNK - PIECE
    kept_first = raw_start // BAND - 1
    last_window = (windows - 1 - kept_first) * SETS
    to_next = remote(projections.at[pl.ds(last_window, SETS)], above,
                     halo_send.at[2], halo_recv.at[2], next_id)

    table_copies = [
        remote(tables.at[quarter], tables.at[quarter], table_send.at[i], table_recv.at[i], device)
        for i, device in enumerate((near_id, far_id, across_id))
    ]
    for copy in table_copies:
        copy.start()

    pieces = CHUNK // PIECE

    def gather_copy(chunk, part, device, held=ext):
        span = pl.ds(chunk * CHUNK + part * PIECE, PIECE)
        number = chunk * pieces + part
        return remote(
            held.at[span], gathered.at[span],
            gather_send.at[number], gather_recv.at[number], device,
        )

    def reduce_copy(chunk, device):
        span = pl.ds(chunk * CHUNK, CHUNK)
        return remote(
            partial.at[span], arrived.at[span],
            reduce_send.at[chunk], reduce_recv.at[chunk], device,
        )

    def send_pair(pair, parts):
        for i in parts:
            gather_copy(2 * pair, i, near_id).start()
            gather_copy(2 * pair + 1, i, far_id).start()

    raw_copies = [
        gather_copy(chunks - 2, 1, near_id, slab), gather_copy(chunks - 1, 0, far_id, slab)
    ]
    for copy in raw_copies:
        copy.start()

    @pl.when(even & has_prev)
    def _():
        pl.semaphore_signal(ready.at[1], inc=1, device_id=prev_id, device_id_type=MESH)
        for copy in to_prev:
            copy.start()

    @pl.when(even & has_next)
    def _():
        pl.semaphore_signal(ready.at[0], inc=1, device_id=next_id, device_id_type=MESH)

    @pl.when(jnp.logical_not(has_prev))
    def _():
        above[...] = jnp.zeros((SETS, width), F32)

    @pl.when(jnp.logical_not(has_next))
    def _():
        ext[pl.ds(rows, BELOW)] = jnp.zeros((BELOW, width), F32)
        refl[:, pl.ds(rows, BELOW)] = jnp.zeros((SETS, BELOW), F32)

    own_refl.wait()
    own_scale_copy.wait()

    def turn(block):
        span = slice(block * BAND, (block + 1) * BAND)
        turned[span, :SETS] = refl[:, span].T

    for block in range(windows):
        turn(block)

    place = lax.broadcasted_iota(jnp.int32, (BAND + 8, 1), 0)
    own_scales = scales_own[...]

    def sweep(index, number):
        offset = set_offset(index)
        base, shift = offset // 8 * 8, offset % 8
        inside = (place >= shift) & (place < BAND + shift)
        span = slice(number * BAND + base, number * BAND + base + BAND + 8)
        blade = jnp.where(inside, turned[span, index : index + 1], 0.0)
        panel = ext[span]
        projection = jnp.sum(blade * panel, axis=0, keepdims=True)
        projection = projection * own_scales[index : index + 1, number : number + 1]
        if number >= kept_first:
            at = (number - kept_first) * SETS + index
            projections[at : at + 1] = projection
        ext[span] = panel - blade * projection

    own_slab.wait()
    early = ((chunks - 3) * CHUNK + PIECE) // BAND
    for index in range(SETS):
        for number in range(index, early):
            sweep(index, number)
    send_pair(chunks // 2 - 2, range(1))
    for index in range(SETS):
        for number in range(early, windows - 1):
            sweep(index, number)
    send_pair(chunks // 2 - 2, range(1, pieces))

    @pl.when(odd & has_prev)
    def _():
        pl.semaphore_wait(ready.at[0], 1)
        for copy in to_prev:
            copy.start()

    fix_rows = (PIECE // BAND + 1) * SETS
    fix_copies = [
        remote(projections.at[pl.ds(i * SETS, fix_rows)], fixes.at[i],
               fix_send.at[i], fix_recv.at[i], device)
        for i, device in enumerate((near_id, far_id))
    ]
    for copy in fix_copies:
        copy.start()
    gather_copy(chunks - 2, 0, near_id).start()

    @pl.when(has_next)
    def _():
        for copy in to_prev:
            copy.wait_recv()

    turn(windows)
    for index in range(SETS):
        sweep(index, windows - 1)

    @pl.when(odd & has_next)
    def _():
        pl.semaphore_wait(ready.at[1], 1)

    gather_copy(chunks - 1, 1, far_id).start()

    @pl.when(has_next)
    def _():
        to_next.start()

    for copy in table_copies:
        copy.wait_recv()
    for i in range(4):
        span = slice(i * width, (i + 1) * width)
        wide[:6, span] = tables[i, :6]
        wide[6:, span] = jnp.where(tables[i, 6:] != 0.0, tables[i, :2], -1.0)
    for i in range(4 * width // BAND):
        tall[i * BAND : (i + 1) * BAND, :SETS] = wide[:, i * BAND : (i + 1) * BAND].T

    def fold(value):
        return jnp.sum(value.reshape(value.shape[0] // 8, 8, value.shape[1]), axis=0)

    def pick(index, ranks_row, start, size):
        depth = 64
        positions = lax.broadcasted_iota(jnp.int32, (depth, 1), 0)

        def step(number, total):
            at = pl.ds(pl.multiple_of(start + number * depth, depth), depth)
            here = (positions + number * depth).astype(F32)
            root = tall[at, 4 + index : 5 + index]
            return total + fold(jnp.where(ranks_row == here, root, 0.0))

        total = lax.fori_loop(0, size // depth, step, jnp.zeros((8, size), F32), unroll=4)
        return jnp.sum(total, axis=0, keepdims=True)

    def weigh(index, start, size):
        depth = 64
        span = slice(start, start + size)
        root = pick(index, wide[index : index + 1, span], start, size)
        pole = wide[2 + index : 3 + index, span]
        living = wide[6 + index : 7 + index, span] < 0.0
        lanes = lax.broadcasted_iota(jnp.int32, (1, BAND), 1)
        places = lax.broadcasted_iota(jnp.int32, (depth, 1), 0)

        def step(number, carry):
            at = pl.ds(pl.multiple_of(start + number * depth, depth), depth)
            own = tall[at, 2 + index : 3 + index]
            own_place = number * depth + places
            total = jnp.zeros((depth, BAND), F32)
            for tile in range(size // BAND):
                part = slice(tile * BAND, (tile + 1) * BAND)
                apart = jnp.abs(pole[:, part] - own)
                between = jnp.where(lanes + tile * BAND == own_place, 1.0, apart)
                logs = jnp.log(jnp.abs(root[:, part] - own) / between)
                total = total + jnp.where(living[:, part], logs, 0.0)
            alive = tall[at, 6 + index : 7 + index] < 0.0
            weight = jnp.exp(0.5 * jnp.sum(total, axis=1, keepdims=True))
            weights[at, index : index + 1] = jnp.where(alive, weight, 0.0)
            return carry

        lax.fori_loop(0, size // depth, step, 0, unroll=4)

    weigh(0, 0, 2 * width)
    weigh(0, 2 * width, 2 * width)
    weigh(1, 0, 4 * width)

    @pl.when(has_prev)
    def _():
        to_next.wait_recv()

    head = lax.broadcasted_iota(jnp.int32, (BAND, 1), 0)
    for index in range(SETS):
        blade = jnp.where(head < set_offset(index), turned[:BAND, index : index + 1], 0.0)
        ext[:BAND] = ext[:BAND] - blade * above[index : index + 1]
        for number in range(index):
            sweep(index, number)
    for pair in reversed(range(chunks // 2 - 2)):
        send_pair(pair, range(pieces))

    def level(index, start, size, store, blocks):
        depth = 64
        roots_of = [tables[block, 4 + index : 5 + index] for block, _ in blocks]
        ranks_of = [
            (within * width + lax.broadcasted_iota(jnp.int32, (1, width), 1)).astype(F32)
            for _, within in blocks
        ]

        def cauchy(step, carry):
            at = pl.ds(pl.multiple_of(step * depth, depth), depth)
            shift = pl.ds(pl.multiple_of(start + step * depth, depth), depth)
            weight = weights[shift, index : index + 1]
            pole = tall[shift, 2 + index : 3 + index]
            dead_rank = tall[shift, 6 + index : 7 + index]
            sums = []
            for number in range(len(blocks)):
                norms, dead = carry[number]
                value = weight / (pole - roots_of[number])
                store[number, at] = value
                norms = norms + fold(value * value)
                dead = dead + fold(jnp.where(dead_rank == ranks_of[number], 1.0, 0.0))
                sums.append((norms, dead))
            return tuple(sums)

        zero = jnp.zeros((8, width), F32)
        sums = lax.fori_loop(0, size // depth, cauchy, ((zero, zero),) * len(blocks), unroll=4)
        scales_of = [
            jnp.where(
                jnp.sum(dead, axis=0, keepdims=True) > 0.0, 0.0,
                1.0 / jnp.sqrt(jnp.sum(norms, axis=0, keepdims=True)),
            )
            for norms, dead in sums
        ]

        def finish(step, carry):
            at = pl.ds(pl.multiple_of(step * depth, depth), depth)
            shift = pl.ds(pl.multiple_of(start + step * depth, depth), depth)
            dead_rank = tall[shift, 6 + index : 7 + index]
            for number in range(len(blocks)):
                store[number, at] = jnp.where(
                    dead_rank == ranks_of[number], 1.0, store[number, at] * scales_of[number]
                )
            return carry

        lax.fori_loop(0, size // depth, finish, 0, unroll=4)

    for group in range(2):
        level(
            0, group * 2 * width, 2 * width, mix_one.at[group],
            [(2 * group, 0), (2 * group + 1, 1)],
        )
    level(1, 0, 4 * width, mix_two, [(quarter, quarter), (near, near), (far, far)])

    for which, (other, kept) in enumerate(((near, 2), (far, 1))):
        for part, source in enumerate((quarter, other)):
            group = source // 2
            at = pl.ds(pl.multiple_of(lax.rem(source, 2) * width, width), width)
            left = jnp.concatenate([mix_one[group, 0, at], mix_one[group, 1, at]], axis=1)
            under = pl.ds(pl.multiple_of(group * 2 * width, width), 2 * width)
            for side, block in enumerate((0, kept)):
                span = (which, slice(part * width, (part + 1) * width), slice(side * width, (side + 1) * width))
                if which == 1 and part == 0 and side == 0:
                    plan_high[span] = plan_high[(0,) + span[1:]]
                    plan_low[span] = plan_low[(0,) + span[1:]]
                    continue
                high, low = halves(mix_two[block, under])
                value = dot3(left, high, low)
                high, low = halves(value)
                plan_high[span] = high
                plan_low[span] = low

    for which in range(2):
        start = raw_start + which * PIECE
        span = slice(start, start + PIECE)
        lines = start + lax.broadcasted_iota(jnp.int32, (SETS, PIECE), 1)
        offsets = 1 + (SETS - 1 - lax.broadcasted_iota(jnp.int32, (SETS, PIECE), 0)) * (
            (BAND - 2) // (SETS - 1)
        )
        blades = []
        for number in range(fix_rows // SETS):
            starts = offsets + (kept_first + which + number) * BAND
            inside = (lines >= starts) & (lines < starts + BAND)
            blades.append(jnp.where(inside, refl[:, span], 0.0))
        fix_copies[which].wait_recv()
        high, low = halves(fixes[which])
        correction = dot3(jnp.concatenate(blades, axis=0).T, high, low)
        raw_copies[which].wait_recv()
        gathered[span] = gathered[span] - correction

    def pair_of(step):
        return jnp.where(step < 2, chunks // 2 - 2 + step, chunks // 2 - 1 - step)

    def merge(step, carry):
        pair = pair_of(step)
        for which in range(2):
            chunk = 2 * pair + which

            gather_copy(chunk, which, near_id if which == 0 else far_id).wait_recv()

            @pl.when(step != 1)
            def _():
                gather_copy(chunk, 1 - which, near_id if which == 0 else far_id).wait_recv()

            span = pl.ds(pl.multiple_of(chunk * CHUNK, CHUNK), CHUNK)
            mine = ext[span]
            left = jnp.concatenate([mine, gathered[span]], axis=1)
            away = slice(width, 2 * width)
            partial[span] = dot3(left, plan_high[which, :, away], plan_low[which, :, away])
            reduce_copy(chunk, far_id if which == 0 else near_id).start()
            home = slice(0, width)
            out[span] = dot3(left, plan_high[which, :, home], plan_low[which, :, home])
        return carry

    lax.fori_loop(0, chunks // 2, merge, 0)

    for chunk in range(chunks):
        for i in range(pieces):
            gather_copy(chunk, i, near_id if chunk % 2 == 0 else far_id).wait_send()
    for copy in table_copies + fix_copies:
        copy.wait_send()

    @pl.when(has_prev)
    def _():
        for copy in to_prev:
            copy.wait_send()

    @pl.when(has_next)
    def _():
        to_next.wait_send()

    def collect(step, carry):
        pair = pair_of(step)
        for which in range(2):
            chunk = 2 * pair + which
            copy = reduce_copy(chunk, far_id if which == 0 else near_id)
            copy.wait_recv()
            span = pl.ds(pl.multiple_of(chunk * CHUNK, CHUNK), CHUNK)
            out[span] = out[span] + arrived[span]
            copy.wait_send()
        return carry

    lax.fori_loop(0, chunks // 2, collect, 0)


def per_device(slab, ranks, poles, roots, flags, reflectors, reflector_scales):
    rows, width = slab.shape
    chunks = rows // CHUNK
    total = rows + BELOW
    kept = (CHUNK // BAND + 2) * SETS
    fix_rows = (PIECE // BAND + 1) * SETS
    anywhere = pl.BlockSpec(memory_space=pl.ANY)
    dma = pltpu.SemaphoreType.DMA
    operands = (slab, ranks, poles, roots, flags, reflectors, reflector_scales)
    held = [pltpu.with_memory_space_constraint(x, pltpu.HBM) for x in operands]
    return pl.pallas_call(
        kernel,
        out_shape=pltpu.VMEM((rows, width), F32),
        in_specs=[anywhere] * 7,
        out_specs=pl.BlockSpec(memory_space=pltpu.VMEM),
        scratch_shapes=[
            pltpu.VMEM((total, width), F32),
            pltpu.VMEM((SETS, total), F32),
            pltpu.VMEM(reflector_scales.shape, F32),
            pltpu.VMEM((total, 128), F32),
            pltpu.VMEM((rows, width), F32),
            pltpu.VMEM((4, 8, width), F32),
            pltpu.VMEM((4 * width, 128), F32),
            pltpu.VMEM((8, 4 * width), F32),
            pltpu.VMEM((2, 2, width), jnp.int32),
            pltpu.VMEM((2, 2, width), F32),
            pltpu.VMEM((4 * width, 128), F32),
            pltpu.VMEM((kept, width), F32),
            pltpu.VMEM((SETS, width), F32),
            pltpu.VMEM((2, fix_rows, width), F32),
            pltpu.VMEM((2, 2, 2 * width, width), F32),
            pltpu.VMEM((3, 4 * width, width), F32),
            pltpu.VMEM((2, 2 * width, 2 * width), BF16),
            pltpu.VMEM((2, 2 * width, 2 * width), BF16),
            pltpu.VMEM((rows, width), F32),
            pltpu.VMEM((rows, width), F32),
            dma((7,)), dma((3,)), dma((3,)), dma((3,)), dma((3,)), dma((2,)), dma((2,)),
            dma((rows // PIECE,)), dma((rows // PIECE,)), dma((chunks,)), dma((chunks,)),
            pltpu.SemaphoreType.REGULAR((2,)),
        ],
        compiler_params=pltpu.CompilerParams(
            collective_id=0, has_side_effects=True, vmem_limit_bytes=48 * 1024 * 1024
        ),
    )(*held)


def solution(mesh):
    return jax.shard_map(
        per_device,
        mesh=mesh,
        in_specs=(
            P("row", "col"),
            P(None, "col"),
            P(None, "col"),
            P(None, "col"),
            P(None, "col"),
            P(None, "row"),
            P(None, "row"),
        ),
        out_specs=P("row", "col"),
        check_vma=False,
    )
```

```python
import functools

import jax
import jax.numpy as jnp
from jax import lax
from jax.experimental import pallas as pl
from jax.experimental.pallas import tpu as pltpu
from jax.sharding import PartitionSpec as P

BAND = 128
SETS = 8
BELOW = 128
CHUNK = 256
PIECE = 128
MESH = pl.DeviceIdType.MESH
F32 = jnp.float32
BF16 = jnp.bfloat16


def set_offset(index):
    return 1 + (SETS - 1 - index) * (BAND - 2) // (SETS - 1)


def halves(value):
    high = value.astype(BF16)
    low = (value - high.astype(F32)).astype(BF16)
    return high, low


def dot(left, right):
    return jnp.dot(left, right, preferred_element_type=F32)


def dot3(left, right_high, right_low):
    high, low = halves(left)
    return dot(high, right_high) + (dot(high, right_low) + dot(low, right_high))


def kernel(
    slab, ranks, poles, roots, flags, reflectors, scales, out,
    ext, refl, scales_own, turned, gathered, tables, tall, wide,
    raw_ints, raw_floats, weights, projections, above, fixes,
    mix_one, mix_two, plan_high, plan_low, partial, arrived,
    local_sems, halo_send, halo_recv, table_send, table_recv, fix_send, fix_recv,
    gather_send, gather_recv, reduce_send, reduce_recv, ready,
):
    rows = slab.shape[0]
    width = slab.shape[1]
    chunks = rows // CHUNK
    windows = rows // BAND
    row = lax.axis_index("row")
    row_size = lax.axis_size("row")
    col = lax.axis_index("col")
    quarter = lax.rem(col, 4)
    quad = col - quarter
    near = quarter + 1 - 2 * lax.rem(quarter, 2)
    far = lax.rem(quarter + 2, 4)
    across = 3 - quarter
    near_id = (row, quad + near)
    far_id = (row, quad + far)
    across_id = (row, quad + across)
    odd = lax.rem(row, 2) == 1
    even = jnp.logical_not(odd)
    has_prev = row > 0
    has_next = row < row_size - 1
    prev_id = (lax.max(row - 1, 0), col)
    next_id = (lax.min(row + 1, row_size - 1), col)

    barrier = pltpu.get_barrier_semaphore()
    for partner in (near_id, far_id, across_id):
        pl.semaphore_signal(barrier, inc=1, device_id=partner, device_id_type=MESH)

    @pl.when(odd & has_prev)
    def _():
        pl.semaphore_signal(barrier, inc=1, device_id=prev_id, device_id_type=MESH)

    @pl.when(odd & has_next)
    def _():
        pl.semaphore_signal(barrier, inc=1, device_id=next_id, device_id_type=MESH)

    own_rows = pl.ds(0, rows)
    own_slab = pltpu.make_async_copy(slab, ext.at[own_rows], local_sems.at[0])
    own_refl = pltpu.make_async_copy(reflectors, refl.at[:, own_rows], local_sems.at[1])
    own_scale_copy = pltpu.make_async_copy(scales, scales_own, local_sems.at[2])
    small = [
        pltpu.make_async_copy(ranks, raw_ints.at[0], local_sems.at[3]),
        pltpu.make_async_copy(flags, raw_ints.at[1], local_sems.at[4]),
        pltpu.make_async_copy(poles, raw_floats.at[0], local_sems.at[5]),
        pltpu.make_async_copy(roots, raw_floats.at[1], local_sems.at[6]),
    ]
    for copy in small:
        copy.start()
    own_refl.start()
    own_scale_copy.start()
    own_slab.start()

    for copy in small:
        copy.wait()
    tables[quarter] = jnp.concatenate(
        [raw_ints[0].astype(F32), raw_floats[0], raw_floats[1], raw_ints[1].astype(F32)], axis=0
    )

    pl.semaphore_wait(
        barrier, 3 + jnp.where(even & has_prev, 1, 0) + jnp.where(even & has_next, 1, 0)
    )

    def remote(source, target, send, recv, device):
        return pltpu.make_async_remote_copy(
            src_ref=source, dst_ref=target, send_sem=send, recv_sem=recv,
            device_id=device, device_id_type=MESH,
        )

    to_prev = [
        remote(reflectors.at[:, pl.ds(0, BELOW)], refl.at[:, pl.ds(rows, BELOW)],
               halo_send.at[0], halo_recv.at[0], prev_id),
        remote(slab.at[pl.ds(0, BELOW)], ext.at[pl.ds(rows, BELOW)],
               halo_send.at[1], halo_recv.at[1], prev_id),
    ]
    raw_start = (chunks - 1) * CHUNK - PIECE
    kept_first = raw_start // BAND - 1
    last_window = (windows - 1 - kept_first) * SETS
    to_next = remote(projections.at[pl.ds(last_window, SETS)], above,
                     halo_send.at[2], halo_recv.at[2], next_id)

    table_copies = [
        remote(tables.at[quarter], tables.at[quarter], table_send.at[i], table_recv.at[i], device)
        for i, device in enumerate((near_id, far_id, across_id))
    ]
    for copy in table_copies:
        copy.start()

    pieces = CHUNK // PIECE

    def gather_copy(chunk, part, device, held=ext):
        span = pl.ds(chunk * CHUNK + part * PIECE, PIECE)
        number = chunk * pieces + part
        return remote(
            held.at[span], gathered.at[span],
            gather_send.at[number], gather_recv.at[number], device,
        )

    def reduce_copy(chunk, device):
        span = pl.ds(chunk * CHUNK, CHUNK)
        return remote(
            partial.at[span], arrived.at[span],
            reduce_send.at[chunk], reduce_recv.at[chunk], device,
        )

    def send_pair(pair, parts):
        for i in parts:
            gather_copy(2 * pair, i, near_id).start()
            gather_copy(2 * pair + 1, i, far_id).start()

    raw_copies = [
        gather_copy(chunks - 2, 1, near_id, slab), gather_copy(chunks - 1, 0, far_id, slab)
    ]
    for copy in raw_copies:
        copy.start()

    @pl.when(even & has_prev)
    def _():
        pl.semaphore_signal(ready.at[1], inc=1, device_id=prev_id, device_id_type=MESH)
        for copy in to_prev:
            copy.start()

    @pl.when(even & has_next)
    def _():
        pl.semaphore_signal(ready.at[0], inc=1, device_id=next_id, device_id_type=MESH)

    @pl.when(jnp.logical_not(has_prev))
    def _():
        above[...] = jnp.zeros((SETS, width), F32)

    @pl.when(jnp.logical_not(has_next))
    def _():
        ext[pl.ds(rows, BELOW)] = jnp.zeros((BELOW, width), F32)
        refl[:, pl.ds(rows, BELOW)] = jnp.zeros((SETS, BELOW), F32)

    own_refl.wait()
    own_scale_copy.wait()

    def turn(block):
        span = slice(block * BAND, (block + 1) * BAND)
        turned[span, :SETS] = refl[:, span].T

    for block in range(windows):
        turn(block)

    place = lax.broadcasted_iota(jnp.int32, (BAND + 8, 1), 0)
    own_scales = scales_own[...]

    def sweep(index, number):
        offset = set_offset(index)
        base, shift = offset // 8 * 8, offset % 8
        inside = (place >= shift) & (place < BAND + shift)
        span = slice(number * BAND + base, number * BAND + base + BAND + 8)
        blade = jnp.where(inside, turned[span, index : index + 1], 0.0)
        panel = ext[span]
        projection = jnp.sum(blade * panel, axis=0, keepdims=True)
        projection = projection * own_scales[index : index + 1, number : number + 1]
        if number >= kept_first:
            at = (number - kept_first) * SETS + index
            projections[at : at + 1] = projection
        ext[span] = panel - blade * projection

    own_slab.wait()
    early = ((chunks - 3) * CHUNK + PIECE) // BAND
    for index in range(SETS):
        for number in range(index, early):
            sweep(index, number)
    send_pair(chunks // 2 - 2, range(1))
    for index in range(SETS):
        for number in range(early, windows - 1):
            sweep(index, number)
    send_pair(chunks // 2 - 2, range(1, pieces))

    @pl.when(odd & has_prev)
    def _():
        pl.semaphore_wait(ready.at[0], 1)
        for copy in to_prev:
            copy.start()

    fix_rows = (PIECE // BAND + 1) * SETS
    fix_copies = [
        remote(projections.at[pl.ds(i * SETS, fix_rows)], fixes.at[i],
               fix_send.at[i], fix_recv.at[i], device)
        for i, device in enumerate((near_id, far_id))
    ]
    for copy in fix_copies:
        copy.start()
    gather_copy(chunks - 2, 0, near_id).start()

    @pl.when(has_next)
    def _():
        for copy in to_prev:
            copy.wait_recv()

    turn(windows)
    for index in range(SETS):
        sweep(index, windows - 1)

    @pl.when(odd & has_next)
    def _():
        pl.semaphore_wait(ready.at[1], 1)

    gather_copy(chunks - 1, 1, far_id).start()

    @pl.when(has_next)
    def _():
        to_next.start()

    for copy in table_copies:
        copy.wait_recv()
    for i in range(4):
        span = slice(i * width, (i + 1) * width)
        wide[:6, span] = tables[i, :6]
        wide[6:, span] = jnp.where(tables[i, 6:] != 0.0, tables[i, :2], -1.0)
    for i in range(4 * width // BAND):
        tall[i * BAND : (i + 1) * BAND, :SETS] = wide[:, i * BAND : (i + 1) * BAND].T

    def fold(value):
        return jnp.sum(value.reshape(value.shape[0] // 8, 8, value.shape[1]), axis=0)

    def pick(index, ranks_row, start, size):
        depth = 64
        positions = lax.broadcasted_iota(jnp.int32, (depth, 1), 0)

        def step(number, total):
            at = pl.ds(pl.multiple_of(start + number * depth, depth), depth)
            here = (positions + number * depth).astype(F32)
            root = tall[at, 4 + index : 5 + index]
            return total + fold(jnp.where(ranks_row == here, root, 0.0))

        total = lax.fori_loop(0, size // depth, step, jnp.zeros((8, size), F32), unroll=4)
        return jnp.sum(total, axis=0, keepdims=True)

    def weigh(index, start, size):
        depth = 64
        span = slice(start, start + size)
        root = pick(index, wide[index : index + 1, span], start, size)
        pole = wide[2 + index : 3 + index, span]
        living = wide[6 + index : 7 + index, span] < 0.0
        lanes = lax.broadcasted_iota(jnp.int32, (1, BAND), 1)
        places = lax.broadcasted_iota(jnp.int32, (depth, 1), 0)

        def step(number, carry):
            at = pl.ds(pl.multiple_of(start + number * depth, depth), depth)
            own = tall[at, 2 + index : 3 + index]
            own_place = number * depth + places
            total = jnp.zeros((depth, BAND), F32)
            for tile in range(size // BAND):
                part = slice(tile * BAND, (tile + 1) * BAND)
                apart = jnp.abs(pole[:, part] - own)
                between = jnp.where(lanes + tile * BAND == own_place, 1.0, apart)
                logs = jnp.log(jnp.abs(root[:, part] - own) / between)
                total = total + jnp.where(living[:, part], logs, 0.0)
            alive = tall[at, 6 + index : 7 + index] < 0.0
            weight = jnp.exp(0.5 * jnp.sum(total, axis=1, keepdims=True))
            weights[at, index : index + 1] = jnp.where(alive, weight, 0.0)
            return carry

        lax.fori_loop(0, size // depth, step, 0, unroll=4)

    def head_sweeps():
        @pl.when(has_prev)
        def _():
            to_next.wait_recv()

        head = lax.broadcasted_iota(jnp.int32, (BAND, 1), 0)
        for index in range(SETS):
            blade = jnp.where(head < set_offset(index), turned[:BAND, index : index + 1], 0.0)
            ext[:BAND] = ext[:BAND] - blade * above[index : index + 1]
            for number in range(index):
                sweep(index, number)
        for pair in reversed(range(chunks // 2 - 2)):
            send_pair(pair, range(pieces))

    weigh(1, 0, 4 * width)
    pl.when(even)(head_sweeps)
    weigh(0, 0, 2 * width)
    weigh(0, 2 * width, 2 * width)
    pl.when(odd)(head_sweeps)

    def level(index, start, size, store, blocks):
        depth = 64
        roots_of = [tables[block, 4 + index : 5 + index] for block, _ in blocks]
        ranks_of = [
            (within * width + lax.broadcasted_iota(jnp.int32, (1, width), 1)).astype(F32)
            for _, within in blocks
        ]

        def cauchy(step, carry):
            at = pl.ds(pl.multiple_of(step * depth, depth), depth)
            shift = pl.ds(pl.multiple_of(start + step * depth, depth), depth)
            weight = weights[shift, index : index + 1]
            pole = tall[shift, 2 + index : 3 + index]
            dead_rank = tall[shift, 6 + index : 7 + index]
            sums = []
            for number in range(len(blocks)):
                norms, dead = carry[number]
                value = weight / (pole - roots_of[number])
                store[number, at] = value
                norms = norms + fold(value * value)
                dead = dead + fold(jnp.where(dead_rank == ranks_of[number], 1.0, 0.0))
                sums.append((norms, dead))
            return tuple(sums)

        zero = jnp.zeros((8, width), F32)
        sums = lax.fori_loop(0, size // depth, cauchy, ((zero, zero),) * len(blocks), unroll=4)
        scales_of = [
            jnp.where(
                jnp.sum(dead, axis=0, keepdims=True) > 0.0, 0.0,
                1.0 / jnp.sqrt(jnp.sum(norms, axis=0, keepdims=True)),
            )
            for norms, dead in sums
        ]

        def finish(step, carry):
            at = pl.ds(pl.multiple_of(step * depth, depth), depth)
            shift = pl.ds(pl.multiple_of(start + step * depth, depth), depth)
            dead_rank = tall[shift, 6 + index : 7 + index]
            for number in range(len(blocks)):
                store[number, at] = jnp.where(
                    dead_rank == ranks_of[number], 1.0, store[number, at] * scales_of[number]
                )
            return carry

        lax.fori_loop(0, size // depth, finish, 0, unroll=4)

    for group in range(2):
        level(
            0, group * 2 * width, 2 * width, mix_one.at[group],
            [(2 * group, 0), (2 * group + 1, 1)],
        )
    level(1, 0, 4 * width, mix_two, [(quarter, quarter), (near, near), (far, far)])

    for which, (other, kept) in enumerate(((near, 2), (far, 1))):
        for part, source in enumerate((quarter, other)):
            group = source // 2
            at = pl.ds(pl.multiple_of(lax.rem(source, 2) * width, width), width)
            left = jnp.concatenate([mix_one[group, 0, at], mix_one[group, 1, at]], axis=1)
            under = pl.ds(pl.multiple_of(group * 2 * width, width), 2 * width)
            for side, block in enumerate((0, kept)):
                span = (which, slice(part * width, (part + 1) * width), slice(side * width, (side + 1) * width))
                if which == 1 and part == 0 and side == 0:
                    plan_high[span] = plan_high[(0,) + span[1:]]
                    plan_low[span] = plan_low[(0,) + span[1:]]
                    continue
                high, low = halves(mix_two[block, under])
                value = dot3(left, high, low)
                high, low = halves(value)
                plan_high[span] = high
                plan_low[span] = low

    for which in range(2):
        start = raw_start + which * PIECE
        span = slice(start, start + PIECE)
        lines = start + lax.broadcasted_iota(jnp.int32, (SETS, PIECE), 1)
        offsets = 1 + (SETS - 1 - lax.broadcasted_iota(jnp.int32, (SETS, PIECE), 0)) * (
            (BAND - 2) // (SETS - 1)
        )
        blades = []
        for number in range(fix_rows // SETS):
            starts = offsets + (kept_first + which + number) * BAND
            inside = (lines >= starts) & (lines < starts + BAND)
            blades.append(jnp.where(inside, refl[:, span], 0.0))
        fix_copies[which].wait_recv()
        high, low = halves(fixes[which])
        correction = dot3(jnp.concatenate(blades, axis=0).T, high, low)
        raw_copies[which].wait_recv()
        gathered[span] = gathered[span] - correction

    def pair_of(step):
        return jnp.where(step < 2, chunks // 2 - 2 + step, chunks // 2 - 1 - step)

    def merge(step, carry):
        pair = pair_of(step)
        for which in range(2):
            chunk = 2 * pair + which

            gather_copy(chunk, which, near_id if which == 0 else far_id).wait_recv()

            @pl.when(step != 1)
            def _():
                gather_copy(chunk, 1 - which, near_id if which == 0 else far_id).wait_recv()

            span = pl.ds(pl.multiple_of(chunk * CHUNK, CHUNK), CHUNK)
            mine = ext[span]
            left = jnp.concatenate([mine, gathered[span]], axis=1)
            away = slice(width, 2 * width)
            partial[span] = dot3(left, plan_high[which, :, away], plan_low[which, :, away])
            reduce_copy(chunk, far_id if which == 0 else near_id).start()
            home = slice(0, width)
            out[span] = dot3(left, plan_high[which, :, home], plan_low[which, :, home])
        return carry

    lax.fori_loop(0, chunks // 2, merge, 0)

    for chunk in range(chunks):
        for i in range(pieces):
            gather_copy(chunk, i, near_id if chunk % 2 == 0 else far_id).wait_send()
    for copy in table_copies + fix_copies:
        copy.wait_send()

    @pl.when(has_prev)
    def _():
        for copy in to_prev:
            copy.wait_send()

    @pl.when(has_next)
    def _():
        to_next.wait_send()

    def collect(step, carry):
        pair = pair_of(step)
        for which in range(2):
            chunk = 2 * pair + which
            copy = reduce_copy(chunk, far_id if which == 0 else near_id)
            copy.wait_recv()
            span = pl.ds(pl.multiple_of(chunk * CHUNK, CHUNK), CHUNK)
            out[span] = out[span] + arrived[span]
            copy.wait_send()
        return carry

    lax.fori_loop(0, chunks // 2, collect, 0)


def per_device(slab, ranks, poles, roots, flags, reflectors, reflector_scales):
    rows, width = slab.shape
    chunks = rows // CHUNK
    total = rows + BELOW
    kept = (CHUNK // BAND + 2) * SETS
    fix_rows = (PIECE // BAND + 1) * SETS
    anywhere = pl.BlockSpec(memory_space=pl.ANY)
    dma = pltpu.SemaphoreType.DMA
    operands = (slab, ranks, poles, roots, flags, reflectors, reflector_scales)
    held = [pltpu.with_memory_space_constraint(x, pltpu.HBM) for x in operands]
    return pl.pallas_call(
        kernel,
        out_shape=pltpu.VMEM((rows, width), F32),
        in_specs=[anywhere] * 7,
        out_specs=pl.BlockSpec(memory_space=pltpu.VMEM),
        scratch_shapes=[
            pltpu.VMEM((total, width), F32),
            pltpu.VMEM((SETS, total), F32),
            pltpu.VMEM(reflector_scales.shape, F32),
            pltpu.VMEM((total, 128), F32),
            pltpu.VMEM((rows, width), F32),
            pltpu.VMEM((4, 8, width), F32),
            pltpu.VMEM((4 * width, 128), F32),
            pltpu.VMEM((8, 4 * width), F32),
            pltpu.VMEM((2, 2, width), jnp.int32),
            pltpu.VMEM((2, 2, width), F32),
            pltpu.VMEM((4 * width, 128), F32),
            pltpu.VMEM((kept, width), F32),
            pltpu.VMEM((SETS, width), F32),
            pltpu.VMEM((2, fix_rows, width), F32),
            pltpu.VMEM((2, 2, 2 * width, width), F32),
            pltpu.VMEM((3, 4 * width, width), F32),
            pltpu.VMEM((2, 2 * width, 2 * width), BF16),
            pltpu.VMEM((2, 2 * width, 2 * width), BF16),
            pltpu.VMEM((rows, width), F32),
            pltpu.VMEM((rows, width), F32),
            dma((7,)), dma((3,)), dma((3,)), dma((3,)), dma((3,)), dma((2,)), dma((2,)),
            dma((rows // PIECE,)), dma((rows // PIECE,)), dma((chunks,)), dma((chunks,)),
            pltpu.SemaphoreType.REGULAR((2,)),
        ],
        compiler_params=pltpu.CompilerParams(
            collective_id=0, has_side_effects=True, vmem_limit_bytes=48 * 1024 * 1024
        ),
    )(*held)


def solution(mesh):
    return jax.shard_map(
        per_device,
        mesh=mesh,
        in_specs=(
            P("row", "col"),
            P(None, "col"),
            P(None, "col"),
            P(None, "col"),
            P(None, "col"),
            P(None, "row"),
            P(None, "row"),
        ),
        out_specs=P("row", "col"),
        check_vma=False,
    )
```
